256 devices in a mesh: rep: 4 (over y_hi, core), fsdp: 64 (over z, y_lo, x).
Axes of the slice: x: 4, y: 4 (y_hi: 2, y_lo: 2; y = y_hi * 2 + y_lo), z: 8, core: 2. Of those that a mesh axis runs over, the one named last changes fastest.
Arguments:
- inputs: bfloat16 [4, 49152, 2304], P('rep', 'fsdp'), may hold values from -6 to 6
- cotangent: bfloat16 [4, 49152, 2304], P('rep', 'fsdp'), may hold values from -6 to 6
- replica_params: float32 [4, 1024, 2, 2304], P('rep', 'fsdp'), as said below
- anchor: float32 [1024, 2, 2304], P('fsdp'), as said below
- momentum: float32 [3, 1024, 2, 768], P(None, 'fsdp', None, 'rep'), may hold values from -2 to 2
- fragment: int32 [1], replicated, may hold values from 0 to 2
Outputs:
- replica_new: float32 [4, 1024, 2, 2304], P('rep', 'fsdp')
- anchor_new: float32 [1024, 2, 2304], P('fsdp')
- momentum_new: float32 [3, 1024, 2, 768], P(None, 'fsdp', None, 'rep')
The draws below stay inside these ranges and needn't reach their ends.
Inputs may be any that keep to these rules, and one draw needn't show every extreme that they name: `replica_params`: each replica's parameters are the anchor plus an independent drift with entries of deviation 0.3. `anchor`: entries of deviation 1.
All inputs are finite; a program needn't handle non-finite values.
Results may differ from the reference program's by a relative error of at most 0.0026.
Values may be sent and summed in bfloat16 or wider, within the bound.
A program may use at most 128 MiB of HBM per device.

```python
import math
import jax
import jax.numpy as jnp
from jax import lax

DW = 2304
HV = 1024
NFRAG = 3
REPLICAS = 4
TOKENS = 49152
FRAGW = 768


def shared_params(key):
    return jax.random.normal(key, (HV, 2, DW), jnp.float32)


def draw_anchor(key, part):
    base = shared_params(key)
    return base


def draw_replica_params(key, part):
    base = shared_params(key)
    key = jax.random.fold_in(key, 7)
    drift = 0.3 * jax.random.normal(key, (REPLICAS, HV, 2, DW), jnp.float32)
    return base[None] + drift


def block_levels(key, shape, pieces, low, top_value):
    level = 1.0
    for position, shards_of in pieces:
        steps = jax.random.uniform(jax.random.fold_in(jax.random.fold_in(key, 6), position), (shards_of,), jnp.float32, low / len(pieces), top_value / len(pieces))
        level = level * jnp.repeat(jnp.exp(steps), shape[position] // shards_of).reshape((-1,) + (1,) * (len(shape) - 1 - position))
    return level


def centred(stream_key, dims, deviation, reach, cuts=(), kind=jnp.bfloat16):
    values = deviation * jax.random.normal(stream_key, dims, jnp.float32)
    if cuts:
        values = values * block_levels(stream_key, dims, cuts, -0.22, 0.18)
    return jnp.clip(values, -reach, reach).astype(kind)


def setup_inputs(seed: int = 0) -> dict:
    key_of = jax.random.split(jax.random.key(seed), 7)
    inputs = centred(key_of[0], (REPLICAS, TOKENS, DW), 1.0, 6.0, ((0, 4), (1, 64)))
    cotangent = centred(key_of[1], (REPLICAS, TOKENS, DW), 1.0, 6.0, ((0, 4), (1, 64)))
    replica_params = draw_replica_params(jax.random.fold_in(key_of[6], 71), 0)
    anchor = draw_anchor(jax.random.fold_in(key_of[6], 71), 0)
    momentum = centred(key_of[4], (NFRAG, HV, 2, FRAGW), 0.3, 2.0, ((1, 64), (3, 4)), jnp.float32)
    fragment = jax.random.randint(key_of[5], (1,), 0, NFRAG).astype(jnp.int32)
    return {"inputs": inputs, "cotangent": cotangent, "replica_params": replica_params, "anchor": anchor, "momentum": momentum, "fragment": fragment}


inner_rate = 0.5
outer_rate = 0.7
outer_momentum = 0.9
norm_epsilon = 1e-06

def inner_step(args):
    inputs_one, cotangent_one, params = args
    wide = inputs_one.astype(jnp.float32)
    normed = (wide * lax.rsqrt(lax.optimization_barrier(jnp.mean(wide * wide, axis=-1, keepdims=True)) + norm_epsilon)).astype(jnp.bfloat16)
    weights16 = params.astype(jnp.bfloat16)
    values = (jnp.dot(normed, weights16[:, 0, :].T, preferred_element_type=jnp.float32) / math.sqrt(DW)).astype(jnp.bfloat16)
    back_values = (jnp.dot(cotangent_one, weights16[:, 1, :].T, preferred_element_type=jnp.float32) / math.sqrt(HV)).astype(jnp.bfloat16)
    grad_value = jnp.dot(back_values.T, normed, preferred_element_type=jnp.float32)
    grad_output = jnp.dot(values.T, cotangent_one, preferred_element_type=jnp.float32)
    grads = jnp.stack([grad_value, grad_output], axis=1) * (1.0 / math.sqrt(TOKENS))
    return params - inner_rate * grads

def reference(inputs, cotangent, replica_params, anchor, momentum, fragment):
    inner = lax.map(inner_step, (inputs, cotangent, replica_params))
    index = fragment[0].astype(jnp.int32)
    offset = (index * FRAGW).astype(jnp.int32)
    anchor_frag = lax.dynamic_slice_in_dim(anchor, offset, FRAGW, 2)
    inner_frag = lax.dynamic_slice_in_dim(inner, offset, FRAGW, 3)
    delta = lax.optimization_barrier(jnp.sum(anchor_frag[None] - inner_frag, axis=0)) / REPLICAS
    old_moment = lax.dynamic_index_in_dim(momentum, index, 0, keepdims=False)
    new_moment = outer_momentum * old_moment + delta
    new_frag = anchor_frag - outer_rate * (delta + outer_momentum * new_moment)
    momentum_new = lax.dynamic_update_index_in_dim(momentum, new_moment, index, 0)
    zero = jnp.zeros((), jnp.int32)
    anchor_new = lax.dynamic_update_slice(anchor, new_frag, (zero, zero, offset))
    spread = jnp.broadcast_to(new_frag[None], (REPLICAS,) + new_frag.shape)
    replica_new = lax.dynamic_update_slice(inner, spread, (zero, zero, zero, offset))
    return (replica_new, anchor_new, momentum_new)
```

```python
import functools
import math

import jax
import jax.numpy as jnp
from jax import lax
from jax.experimental import pallas as pl
from jax.experimental.pallas import tpu as pltpu
from jax.sharding import PartitionSpec as P

DW = 2304
HV = 1024
NFRAG = 3
FRAGW = DW // NFRAG
TOKENS = 49152
ROWS = 16
TOK = 768
PAIR = 2 * TOK
CZ = 1024
CY = DW - CZ
Z, Y, X = 8, 2, 4

inner_rate = 0.5
outer_rate = 0.7
outer_momentum = 0.9
norm_epsilon = 1e-06

MESH = pl.DeviceIdType.MESH
F32 = jnp.float32
BF16 = jnp.bfloat16
ZS = pl.ds(0, CZ)
YS = pl.ds(CZ, CY)
ORDER = (4, 3, 5, 2, 6, 1, 7, 0)


def kernel(inp, cot, params, anchor, moment, frag, inner_o, delta_o, moms_o,
           toks, own, wts, wown, vals, grad, rz, sz, ry, sy, r2, fs, fr, fx, xs, osend, orecv, moms,
           load_s, tok_s, tok_r, fwd_s, fwd_r, wx_s, wx_r, ay_s, ay_r, az_s, az_r, bz_s, bz_r, by_s, by_r,
           cz_s, cz_r, cy_s, cy_r, dz_s, dz_r, dy_s, dy_r, ex_s, ex_r, om_s, om_r, of_s, of_r):
    rep = lax.axis_index("rep")
    f = lax.axis_index("fsdp")
    hi, c = rep // 2, rep % 2
    z, y, x = f // 8, (f // 4) % 2, f % 4
    kx, xh = x % 2, x // 2
    nat = 1 - (c + kx) % 2
    is_nat = nat == 1
    yo = 1 - y

    def fid(zz, yy, xx):
        return (zz % Z) * 8 + yy * 4 + xx % X

    def zat(offset):
        return (z + offset) % Z

    sib = (2 * hi + 1 - c, f)
    zdev = ((rep, fid(z + 1, y, x)), (rep, fid(z + 7, y, x)))
    ydev = (rep, fid(z, yo, x))
    peers = (sib, (2 * (1 - hi) + c, f), (2 * (1 - hi) + 1 - c, f))

    pending = []

    def send(src, dst, ssem, rsem, dev):
        cp = pltpu.make_async_remote_copy(src_ref=src, dst_ref=dst, send_sem=ssem, recv_sem=rsem,
                                          device_id=dev, device_id_type=MESH)
        cp.start()
        pending.append(cp)
        return cp

    def recv(region, ssem, rsem):
        pltpu.make_async_remote_copy(src_ref=region, dst_ref=region, send_sem=ssem, recv_sem=rsem,
                                     device_id=ydev, device_id_type=MESH).wait_recv()

    loads = []
    for j in range(6):
        rows = pl.ds(128 * j, 128)
        cp = pltpu.make_async_copy(inp.at[0, rows, :], own.at[rows, :], load_s.at[0, j])
        cp.start()
        loads.append(cp)

    @pl.when(is_nat)
    def _():
        for j in range(6):
            rows = pl.ds(128 * j, 128)
            pltpu.make_async_copy(cot.at[0, rows, :], toks.at[1, rows, :], load_s.at[1, j]).start()

    wown[...] = params[...].astype(BF16)
    moms[rep] = moment[...]

    barrier = pltpu.get_barrier_semaphore()
    group = [(2 * hi + (c + dc) % 2, fid(z, y, x + dx)) for dx in range(4) for dc in range(2) if dx or dc]
    group += [zdev[0], zdev[1], ydev, peers[1], peers[2]]
    for dev in group:
        pl.semaphore_signal(barrier, inc=1, device_id=dev, device_id_type=MESH)
    pl.semaphore_wait(barrier, len(group))

    for d in range(2):
        xd = c + 2 * d
        same = jnp.logical_and(xd == x, xh == c)
        dev = (2 * hi + xh, fid(z, y, xd))
        here = wts.at[:, z, y, kx, :, :]

        @pl.when(jnp.logical_not(same))
        def _(dev=dev, here=here, d=d):
            pltpu.make_async_remote_copy(src_ref=wown, dst_ref=here, send_sem=wx_s.at[d], recv_sem=wx_r.at[kx],
                                         device_id=dev, device_id_type=MESH).start()

        @pl.when(same)
        def _(here=here, d=d):
            pltpu.make_async_copy(wown, here, wx_s.at[d]).start()

    d0 = (nat * sib[0] + (1 - nat) * rep, fid(z, y, x + (1 - nat)))
    d1 = (sib[0], fid(z, y, x + 3 * (1 - nat)))

    def token_send(a, j):
        far = 768 + 256 * j if j < 3 else 768 + 256 * (j - 3) + 128
        rows = pl.ds(pl.multiple_of(nat * 128 * j + (1 - nat) * far, 128), 128)
        slot = j if j < 3 else j + 3 * (1 - nat)
        mine = pl.ds(128 * j, 128)
        src = own.at[mine, :] if a == 0 else cot.at[0, mine, :]
        send(src, toks.at[a, rows, :], tok_s.at[a, j], tok_r.at[a, slot], d0 if j < 3 else d1)

    def normalize(j):
        loads[j].wait()

        def body(i, carry):
            rows = pl.ds(pl.multiple_of(128 * j + 32 * i, 32), 32)
            wide = own[rows, :].astype(F32)
            out = (wide * lax.rsqrt(jnp.mean(wide * wide, axis=-1, keepdims=True) + norm_epsilon)).astype(BF16)
            own[rows, :] = out

            @pl.when(is_nat)
            def _():
                toks[0, rows, :] = out
            return carry
        lax.fori_loop(0, 4, body, 0)

    def tokens_out(js):
        for j in js:
            token_send(1, j)
        for j in js:
            normalize(j)
            token_send(0, j)

    for t, dev in enumerate(peers):
        send(moms.at[rep], moms.at[rep], om_s.at[t], om_r.at[t], dev)

    tokens_out((0, 3))

    for xl in range(2):
        here = wts.at[:, z, y, xl, :, :]
        same = jnp.logical_and(jnp.logical_and(is_nat, xh == c), kx == xl)

        @pl.when(jnp.logical_not(same))
        def _(here=here, xl=xl):
            recv(here, wx_s.at[0], wx_r.at[xl])

        @pl.when(same)
        def _(here=here):
            pltpu.make_async_copy(wown, here, wx_s.at[xh]).wait()

    def ga_region(k, off):
        return wts.at[k, zat(off), :, :, :, ZS]

    def ga_send(d, k, s):
        r = ga_region(k, -(s - 1) if d == 0 else s - 1)
        send(r, r, az_s.at[d, k, s - 1], az_r.at[d, k, s - 1], zdev[d])

    def ga_recv(d, k, s):
        recv(ga_region(k, -s if d == 0 else s), az_s.at[d, k, s - 1], az_r.at[d, k, s - 1])

    def gb_region(off, s, d):
        if s == 4:
            return wts.at[d, zat(off), y, :, :, YS]
        return wts.at[:, zat(off), y, :, :, YS]

    def gb_send(d, s):
        r = gb_region(-(s - 1) if d == 0 else s - 1, s, d)
        send(r, r, bz_s.at[d, s - 1], bz_r.at[d, s - 1], zdev[d])

    def gb_recv(d, s):
        recv(gb_region(-s if d == 0 else s, s, d), bz_s.at[d, s - 1], bz_r.at[d, s - 1])

    def by_region(slot, yy):
        if slot >= 7:
            return wts.at[slot - 7, zat(4), yy, :, :, YS]
        off = -slot if slot < 4 else slot - 3
        return wts.at[:, zat(off), yy, :, :, YS]

    def gby_send(slot):
        r = by_region(slot, y)
        send(r, r, by_s.at[slot], by_r.at[slot], ydev)

    def gby_recv(slot):
        recv(by_region(slot, yo), by_s.at[slot], by_r.at[slot])

    r = wts.at[:, z, y, :, :, ZS]
    send(r, r, ay_s.at[0], ay_r.at[0], ydev)
    gb_send(0, 1)
    gb_send(1, 1)
    gby_send(0)
    recv(wts.at[:, z, yo, :, :, ZS], ay_s.at[0], ay_r.at[0])
    for k in range(2):
        ga_send(0, k, 1)
        ga_send(1, k, 1)
    tokens_out((1, 4))
    for s in range(1, 4):
        for d in range(2):
            gb_recv(d, s)
            gb_send(d, s + 1)
            gby_send(s + 3 * d)
        for k in range(2):
            for d in range(2):
                ga_recv(d, k, s)
                if s < 3 or d == k:
                    ga_send(d, k, s + 1)
        if s == 1:
            tokens_out((2, 5))
    for d in range(2):
        gb_recv(d, 4)
        gby_send(7 + d)
    for d in range(2):
        ga_recv(d, d, 4)

    got = nat * 0 + (1 - nat) * 128
    give = nat * 128 + (1 - nat) * 0

    def forward(j):
        for a in range(2):
            rows = pl.ds(pl.multiple_of(768 + 256 * j + got, 128), 128)
            r = toks.at[a, rows, :]
            recv(r, tok_s.at[a, 0], tok_r.at[a, nat * j + (1 - nat) * (6 + j)])
            send(r, r, fwd_s.at[a, j], fwd_r.at[a, j], sib)

    def forwarded(j):
        for a in range(2):
            rows = pl.ds(pl.multiple_of(768 + 256 * j + give, 128), 128)
            recv(toks.at[a, rows, :], fwd_s.at[a, j], fwd_r.at[a, j])

    def values(group):
        def body(i, carry):
            k, rg = i // 2, i % 2
            tk = pl.ds(256 * group, 256)
            lhs = wts[k, pl.ds(4 * rg, 4), :, :, :, :].reshape(256, DW)
            out = lax.dot_general(lhs, toks[k, tk, :], (((1,), (1,)), ((), ())), preferred_element_type=F32)
            scale = jnp.where(k == 0, 1.0 / math.sqrt(DW), 1.0 / math.sqrt(HV)).astype(F32)
            vals[k, pl.ds(4 * rg, 4), :, :, :, tk] = (out * scale).astype(BF16).reshape(4, 2, 2, 16, 256)
            return carry
        lax.fori_loop(0, 4, body, 0)

    forward(0)
    forward(1)
    for slot in range(9):
        gby_recv(slot)

    @pl.when(is_nat)
    def _():
        for j in range(6):
            rows = pl.ds(128 * j, 128)
            pltpu.make_async_copy(cot.at[0, rows, :], toks.at[1, rows, :], load_s.at[1, j]).wait()

    @pl.when(jnp.logical_not(is_nat))
    def _():
        for j in range(6):
            for a in range(2):
                recv(toks.at[a, pl.ds(128 * j, 128), :], tok_s.at[a, 0], tok_r.at[a, j])

    values(0)
    values(1)
    values(2)
    forwarded(0)
    values(3)
    forward(2)
    forwarded(1)
    values(4)
    forwarded(2)
    values(5)

    def grad_z(offs):
        def body(k, carry):
            lhs = jnp.concatenate([vals[1 - k, zat(o)].reshape(64, PAIR) for o in offs], axis=0)
            out = jnp.dot(lhs, toks[k, :, 0:CZ], preferred_element_type=F32)
            for i, o in enumerate(offs):
                grad[k, zat(o), :, :, :, 0:CZ] = out[64 * i:64 * i + 64].reshape(2, 2, 16, CZ)
            return carry
        lax.fori_loop(0, 2, body, 0)

    def grad_y(offs, yy):
        def body(k, carry):
            lhs = jnp.concatenate([vals[1 - k, zat(o), yy].reshape(32, PAIR) for o in offs], axis=0)
            out = jnp.dot(lhs, toks[k, :, CZ:DW], preferred_element_type=F32)
            for i, o in enumerate(offs):
                grad[k, zat(o), yy, :, :, CZ:DW] = out[32 * i:32 * i + 32].reshape(2, 16, CY)
            return carry
        lax.fori_loop(0, 2, body, 0)

    def rz_first(slot, d, k, s, off):
        sz[slot] = grad[k, zat(off), :, :, :, 0:CZ].astype(BF16)
        send(sz.at[slot], rz.at[d, k, s - 1], cz_s.at[d, k, s - 1], cz_r.at[d, k, s - 1], zdev[d])

    def rz_hop(d, k, s):
        got = rz.at[d, k, s - 1]
        recv(got, cz_s.at[d, k, s - 1], cz_r.at[d, k, s - 1])
        off = 4 - s if d == 0 else s - 4
        rz[d, k, s - 1] = (rz[d, k, s - 1].astype(F32) + grad[k, zat(off), :, :, :, 0:CZ]).astype(BF16)
        send(got, rz.at[d, k, s], cz_s.at[d, k, s], cz_r.at[d, k, s], zdev[d])

    def ry_send(i):
        sy[i] = grad[:, zat(ORDER[i]), yo, :, :, CZ:DW].astype(BF16)
        send(sy.at[i], ry.at[i], cy_s.at[i], cy_r.at[i], ydev)

    def ry_recv(i):
        recv(ry.at[i], cy_s.at[i], cy_r.at[i])

    def r2_first():
        ry_recv(0)
        ry[0] = (ry[0].astype(F32) + grad[:, zat(4), y, :, :, CZ:DW]).astype(BF16)
        for d in range(2):
            send(ry.at[0, d], r2.at[d, 0, d], dz_s.at[d, 0], dz_r.at[d, 0], zdev[d])

    def r2_hop(d, s):
        off = 4 - s if d == 0 else s - 4
        i = ORDER.index(off % Z)
        ry_recv(i)
        if s == 1:
            recv(r2.at[d, 0, d], dz_s.at[d, 0], dz_r.at[d, 0])
            r2[d, 0, 1 - d] = (ry[i, 1 - d].astype(F32) + grad[1 - d, zat(off), y, :, :, CZ:DW]).astype(BF16)
            r2[d, 0, d] = (r2[d, 0, d].astype(F32) + ry[i, d].astype(F32)
                           + grad[d, zat(off), y, :, :, CZ:DW]).astype(BF16)
        else:
            recv(r2.at[d, s - 1], dz_s.at[d, s - 1], dz_r.at[d, s - 1])
            for k in range(2):
                r2[d, s - 1, k] = (r2[d, s - 1, k].astype(F32) + ry[i, k].astype(F32)
                                   + grad[k, zat(off), y, :, :, CZ:DW]).astype(BF16)
        send(r2.at[d, s - 1], r2.at[d, s], dz_s.at[d, s], dz_r.at[d, s], zdev[d])

    def owner_send(part, cols):
        for xl in range(2):
            xo = 2 * c + xl
            same = jnp.logical_and(xo == x, kx == c)
            src = fx.at[xl, :, :, cols]
            dst = xs.at[xh, :, :, cols]
            dev = (2 * hi + kx, fid(z, y, xo))

            @pl.when(jnp.logical_not(same))
            def _(src=src, dst=dst, dev=dev, xl=xl):
                pltpu.make_async_remote_copy(src_ref=src, dst_ref=dst, send_sem=ex_s.at[part, xl],
                                             recv_sem=ex_r.at[part, xh], device_id=dev, device_id_type=MESH).start()

            @pl.when(same)
            def _(src=src, dst=dst, xl=xl):
                pltpu.make_async_copy(src, dst, ex_s.at[part, xl]).start()

    def owner_wait(part, cols):
        for d in range(2):
            region = xs.at[d, :, :, cols]
            same = jnp.logical_and(is_nat, jnp.logical_and(xh == c, xh == d))

            @pl.when(jnp.logical_not(same))
            def _(region=region, d=d):
                recv(region, ex_s.at[part, 0], ex_r.at[part, d])
        for xl in range(2):
            same = jnp.logical_and(2 * c + xl == x, kx == c)
            src = fx.at[xl, :, :, cols]
            dst = xs.at[xh, :, :, cols]

            @pl.when(jnp.logical_not(same))
            def _(src=src, xl=xl):
                pltpu.make_async_remote_copy(src_ref=src, dst_ref=src, send_sem=ex_s.at[part, xl],
                                             recv_sem=ex_r.at[part, 0], device_id=ydev,
                                             device_id_type=MESH).wait_send()

            @pl.when(same)
            def _(src=src, dst=dst, xl=xl):
                pltpu.make_async_copy(src, dst, ex_s.at[part, xl]).wait()

    grad_z((4, 3))
    rz_first(0, 0, 0, 1, 4)
    rz_first(1, 1, 1, 1, 4)
    rz_first(2, 0, 1, 2, 3)
    grad_z((5, 2))
    rz_first(3, 1, 0, 2, 5)
    grad_y((4, 3, 5, 2), yo)
    for i in range(4):
        ry_send(i)
    grad_z((6, 1))
    rz_hop(0, 0, 1)
    rz_hop(1, 1, 1)
    grad_y((6, 1, 7, 0), yo)
    for i in range(4, 8):
        ry_send(i)
    grad_y((4, 3, 5, 2), y)
    rz_hop(0, 1, 2)
    rz_hop(1, 0, 2)
    r2_first()
    grad_z((7, 0))
    rz_hop(0, 0, 2)
    rz_hop(1, 1, 2)
    grad_y((6, 1, 7, 0), y)
    r2_hop(0, 1)
    r2_hop(1, 1)
    rz_hop(0, 1, 3)
    rz_hop(1, 0, 3)
    rz_hop(0, 0, 3)
    rz_hop(1, 1, 3)
    r2_hop(0, 2)
    r2_hop(1, 2)
    for d in range(2):
        for k in range(2):
            recv(rz.at[d, k, 3], cz_s.at[d, k, 3], cz_r.at[d, k, 3])
    for k in range(2):
        fs[k] = (grad[k, z, yo, :, :, 0:CZ] + rz[0, k, 3, yo].astype(F32)) + rz[1, k, 3, yo].astype(F32)
    send(fs, fr, dy_s.at[0], dy_r.at[0], ydev)
    for k in range(2):
        mine = (grad[k, z, y, :, :, 0:CZ] + rz[0, k, 3, y].astype(F32)) + rz[1, k, 3, y].astype(F32)
        for xl in range(2):
            fx[xl, k, :, 0:CZ] = mine[xl]
    r2_hop(0, 3)
    r2_hop(1, 3)
    recv(fr, dy_s.at[0], dy_r.at[0])
    for k in range(2):
        for xl in range(2):
            fx[xl, k, :, 0:CZ] = fx[xl, k, :, 0:CZ] + fr[k, xl]
    owner_send(0, ZS)
    ry_recv(7)
    for d in range(2):
        recv(r2.at[d, 3], dz_s.at[d, 3], dz_r.at[d, 3])
    for k in range(2):
        mine = ((grad[k, z, y, :, :, CZ:DW] + ry[7, k].astype(F32))
                + (r2[0, 3, k].astype(F32) + r2[1, 3, k].astype(F32)))
        for xl in range(2):
            fx[xl, k, :, CZ:DW] = mine[xl]
    owner_send(1, YS)
    owner_wait(0, ZS)
    owner_wait(1, YS)

    scale = inner_rate / math.sqrt(TOKENS)
    inner_o[...] = params[...] - scale * (xs[0] + xs[1])
    index = frag[0]
    pick = [inner_o[:, :, FRAGW * i:FRAGW * (i + 1)] for i in range(NFRAG)]
    osend[...] = jnp.where(index == 0, pick[0], jnp.where(index == 1, pick[1], pick[2]))
    for t, dev in enumerate(peers):
        send(osend, orecv.at[t], of_s.at[t], of_r.at[t], dev)
    for t in range(3):
        prep = (sib[0], peers[1][0], peers[2][0])[t]
        recv(moms.at[prep], om_s.at[t], om_r.at[t])
    moms_o[...] = moms[...]
    for t in range(3):
        recv(orecv.at[t], of_s.at[t], of_r.at[t])
    base = anchor[...]
    delta_o[...] = (((base - osend[...]) + (base - orecv[0])) + ((base - orecv[1]) + (base - orecv[2]))) * 0.25

    for d in range(2):
        xd = c + 2 * d
        same = jnp.logical_and(xd == x, xh == c)

        @pl.when(jnp.logical_not(same))
        def _(d=d):
            pltpu.make_async_remote_copy(src_ref=wown, dst_ref=wown, send_sem=wx_s.at[d], recv_sem=wx_r.at[0],
                                         device_id=ydev, device_id_type=MESH).wait_send()
    for cp in pending:
        cp.wait_send()


def window(inp, cot, params, anchor, moment, frag):
    dma = pltpu.SemaphoreType.DMA
    vmem = pltpu.VMEM
    both = lambda *shape: [dma(shape), dma(shape)]
    scratch = [
        vmem((2, PAIR, DW), BF16),
        vmem((TOK, DW), BF16),
        vmem((2, Z, Y, 2, ROWS, DW), BF16),
        vmem((2, ROWS, DW), BF16),
        vmem((2, Z, Y, 2, ROWS, PAIR), BF16),
        vmem((2, Z, Y, 2, ROWS, DW), F32),
        vmem((2, 2, 4, Y, 2, ROWS, CZ), BF16),
        vmem((4, Y, 2, ROWS, CZ), BF16),
        vmem((8, 2, 2, ROWS, CY), BF16),
        vmem((8, 2, 2, ROWS, CY), BF16),
        vmem((2, 4, 2, 2, ROWS, CY), BF16),
        vmem((2, 2, ROWS, CZ), F32),
        vmem((2, 2, ROWS, CZ), F32),
        vmem((2, 2, ROWS, DW), F32),
        vmem((2, 2, ROWS, DW), F32),
        vmem((2, ROWS, FRAGW), F32),
        vmem((3, 2, ROWS, FRAGW), F32),
        vmem((4, 2, ROWS, 256), F32),
        dma((2, 6)),
        dma((2, 6)), dma((2, 9)),
        *both(2, 3),
        *both(2),
        *both(1),
        *both(2, 2, 4),
        *both(2, 4),
        *both(9),
        *both(2, 2, 4),
        *both(8),
        *both(2, 4),
        *both(1),
        *both(2, 2),
        *both(3),
        *both(3),
    ]
    whole = pl.BlockSpec(memory_space=pltpu.VMEM)
    return pl.pallas_call(
        kernel,
        out_shape=(
            jax.ShapeDtypeStruct((2, ROWS, DW), F32),
            jax.ShapeDtypeStruct((2, ROWS, FRAGW), F32),
            jax.ShapeDtypeStruct((4, 2, ROWS, 256), F32),
        ),
        in_specs=[pl.BlockSpec(memory_space=pl.ANY)] * 2 + [whole] * 3 + [pl.BlockSpec(memory_space=pltpu.SMEM)],
        out_specs=(whole, whole, whole),
        scratch_shapes=scratch,
        cost_estimate=pl.CostEstimate(flops=4 * 2 * TOK * DW * HV, bytes_accessed=10**7, transcendentals=TOK),
        compiler_params=pltpu.CompilerParams(
            collective_id=1, has_side_effects=True, vmem_limit_bytes=58 * 2**20
        ),
    )(inp, cot, params, anchor, moment, frag)


def per_device(inputs, cotangent, replica_params, anchor, momentum, fragment):
    index = fragment[0]
    offset = index * FRAGW
    params = jnp.transpose(replica_params[0], (1, 0, 2))
    anchor_frag = lax.dynamic_slice_in_dim(anchor, offset, FRAGW, 2)
    piece = lax.dynamic_index_in_dim(momentum, index, 0, keepdims=False)
    padded = jnp.pad(jnp.transpose(piece, (1, 0, 2)), ((0, 0), (0, 0), (0, 256 - FRAGW // 4)))
    inner, delta, moms = window(
        inputs, cotangent, params, jnp.transpose(anchor_frag, (1, 0, 2)), padded, fragment
    )
    quarter = FRAGW // 4
    old = jnp.concatenate([moms[r, :, :, :quarter] for r in range(4)], axis=-1)
    new_moment = jnp.transpose(outer_momentum * old + delta, (1, 0, 2))
    delta = jnp.transpose(delta, (1, 0, 2))
    new_frag = anchor_frag - outer_rate * (delta + outer_momentum * new_moment)
    mine = lax.dynamic_slice_in_dim(new_moment, lax.axis_index("rep") * quarter, quarter, 2)
    zero = jnp.zeros((), jnp.int32)
    momentum_new = lax.dynamic_update_index_in_dim(momentum, mine, index, 0)
    anchor_new = lax.dynamic_update_slice(anchor, new_frag, (zero, zero, offset))
    inner = jnp.transpose(inner, (1, 0, 2))
    replica_new = lax.dynamic_update_slice(inner, new_frag, (zero, zero, offset))
    return (replica_new[None], anchor_new, momentum_new)


def solution(mesh):
    return jax.shard_map(
        per_device,
        mesh=mesh,
        in_specs=(
            P("rep", "fsdp", None),
            P("rep", "fsdp", None),
            P("rep", "fsdp", None, None),
            P("fsdp", None, None),
            P(None, "fsdp", None, "rep"),
            P(),
        ),
        out_specs=(
            P("rep", "fsdp", None, None),
            P("fsdp", None, None),
            P(None, "fsdp", None, "rep"),
        ),
        check_vma=False,
    )
```

```python
import functools
import math

import jax
import jax.numpy as jnp
from jax import lax
from jax.experimental import pallas as pl
from jax.experimental.pallas import tpu as pltpu
from jax.sharding import PartitionSpec as P

DW = 2304
HV = 1024
NFRAG = 3
FRAGW = DW // NFRAG
QUARTER = FRAGW // 4
TOKENS = 49152
ROWS = 16
TOK = 768
PAIR = 2 * TOK
CZ = 1024
CY = DW - CZ
A0, B0, C0 = 0, 512, 1408
Z, Y, X = 8, 2, 4

inner_rate = 0.5
outer_rate = 0.7
outer_momentum = 0.9
norm_epsilon = 1e-06

MESH = pl.DeviceIdType.MESH
F32 = jnp.float32
BF16 = jnp.bfloat16
ZS = pl.ds(0, CZ)
YS = pl.ds(CZ, CY)
ORDER = (4, 3, 5, 2, 6, 1, 7, 0)


def kernel(inp, cot, params, anchor, moment, frag, inner_o, frag_o, moms_o,
           toks, own, wts, wown, vals, grad, rz, sz, ry, sy, r2, fs, fr, gs, gr, sc, fc, fx, xs, osend, orecv, moms,
           load_s, tok_s, tok_r, fwd_s, fwd_r, wx_s, wx_r, ay_s, ay_r, az_s, az_r, bz_s, bz_r, by_s, by_r,
           cz_s, cz_r, cy_s, cy_r, dz_s, dz_r, dy_s, dy_r, ex_s, ex_r, om_s, om_r, of_s, of_r):
    rep = lax.axis_index("rep")
    f = lax.axis_index("fsdp")
    hi, c = rep // 2, rep % 2
    z, y, x = f // 8, (f // 4) % 2, f % 4
    kx, xh = x % 2, x // 2
    nat = 1 - (c + kx) % 2
    is_nat = nat == 1
    yo = 1 - y

    def fid(zz, yy, xx):
        return (zz % Z) * 8 + yy * 4 + xx % X

    def zat(offset):
        return (z + offset) % Z

    sib = (2 * hi + 1 - c, f)
    zdev = ((rep, fid(z + 1, y, x)), (rep, fid(z + 7, y, x)))
    ydev = (rep, fid(z, yo, x))
    peers = (sib, (2 * (1 - hi) + c, f), (2 * (1 - hi) + 1 - c, f))

    pending = []

    def send(src, dst, ssem, rsem, dev):
        cp = pltpu.make_async_remote_copy(src_ref=src, dst_ref=dst, send_sem=ssem, recv_sem=rsem,
                                          device_id=dev, device_id_type=MESH)
        cp.start()
        pending.append(cp)
        return cp

    def recv(region, ssem, rsem):
        pltpu.make_async_remote_copy(src_ref=region, dst_ref=region, send_sem=ssem, recv_sem=rsem,
                                     device_id=ydev, device_id_type=MESH).wait_recv()

    barrier = pltpu.get_barrier_semaphore()
    group = [(2 * hi + (c + dc) % 2, fid(z, y, x + dx)) for dx in range(4) for dc in range(2) if dx or dc]
    group += [zdev[0], zdev[1], ydev, peers[1], peers[2]]
    for dev in group:
        pl.semaphore_signal(barrier, inc=1, device_id=dev, device_id_type=MESH)

    loads = []
    for j in range(6):
        rows = pl.ds(128 * j, 128)
        cp = pltpu.make_async_copy(inp.at[0, rows, :], own.at[rows, :], load_s.at[0, j])
        cp.start()
        loads.append(cp)

    @pl.when(is_nat)
    def _():
        for j in range(6):
            rows = pl.ds(128 * j, 128)
            pltpu.make_async_copy(cot.at[0, rows, :], toks.at[1, rows, :], load_s.at[1, j]).start()

    index = frag[0]
    for k in range(2):
        wown[k] = params[0, :, k, :].astype(BF16)
        moms[rep, k] = moment[index, :, k, :]
    pl.semaphore_wait(barrier, len(group))

    for d in range(2):
        xd = c + 2 * d
        same = jnp.logical_and(xd == x, xh == c)
        dev = (2 * hi + xh, fid(z, y, xd))
        here = wts.at[:, z, y, kx, :, :]

        @pl.when(jnp.logical_not(same))
        def _(dev=dev, here=here, d=d):
            pltpu.make_async_remote_copy(src_ref=wown, dst_ref=here, send_sem=wx_s.at[d], recv_sem=wx_r.at[kx],
                                         device_id=dev, device_id_type=MESH).start()

        @pl.when(same)
        def _(here=here, d=d):
            pltpu.make_async_copy(wown, here, wx_s.at[d]).start()

    d0 = (nat * sib[0] + (1 - nat) * rep, fid(z, y, x + (1 - nat)))
    d1 = (sib[0], fid(z, y, x + 3 * (1 - nat)))

    def token_send(a, j):
        far = 768 + 256 * j if j < 3 else 768 + 256 * (j - 3) + 128
        rows = pl.ds(pl.multiple_of(nat * 128 * j + (1 - nat) * far, 128), 128)
        slot = j if j < 3 else j + 3 * (1 - nat)
        mine = pl.ds(128 * j, 128)
        src = own.at[mine, :] if a == 0 else cot.at[0, mine, :]
        send(src, toks.at[a, rows, :], tok_s.at[a, j], tok_r.at[a, slot], d0 if j < 3 else d1)

    def normalize(j):
        loads[j].wait()

        def body(i, carry):
            rows = pl.ds(pl.multiple_of(128 * j + 32 * i, 32), 32)
            wide = own[rows, :].astype(F32)
            out = (wide * lax.rsqrt(jnp.mean(wide * wide, axis=-1, keepdims=True) + norm_epsilon)).astype(BF16)
            own[rows, :] = out

            @pl.when(is_nat)
            def _():
                toks[0, rows, :] = out
            return carry
        lax.fori_loop(0, 4, body, 0)

    def tokens_out(js):
        for j in js:
            token_send(1, j)
            token_send(0, j)

    for j in (0, 3):
        token_send(1, j)
    for j in (0, 3):
        normalize(j)
        token_send(0, j)
    for t, dev in enumerate(peers):
        send(moms.at[rep], moms.at[rep], om_s.at[t], om_r.at[t], dev)

    for xl in range(2):
        here = wts.at[:, z, y, xl, :, :]
        same = jnp.logical_and(jnp.logical_and(is_nat, xh == c), kx == xl)

        @pl.when(jnp.logical_not(same))
        def _(here=here, xl=xl):
            recv(here, wx_s.at[0], wx_r.at[xl])

        @pl.when(same)
        def _(here=here):
            pltpu.make_async_copy(wown, here, wx_s.at[xh]).wait()

    def ga_region(k, off):
        return wts.at[k, zat(off), :, :, :, ZS]

    def ga_send(d, k, s):
        r = ga_region(k, -(s - 1) if d == 0 else s - 1)
        send(r, r, az_s.at[d, k, s - 1], az_r.at[d, k, s - 1], zdev[d])

    def ga_recv(d, k, s):
        recv(ga_region(k, -s if d == 0 else s), az_s.at[d, k, s - 1], az_r.at[d, k, s - 1])

    def gb_region(off, s, d):
        if s == 4:
            return wts.at[d, zat(off), y, :, :, YS]
        return wts.at[:, zat(off), y, :, :, YS]

    def gb_send(d, s):
        r = gb_region(-(s - 1) if d == 0 else s - 1, s, d)
        send(r, r, bz_s.at[d, s - 1], bz_r.at[d, s - 1], zdev[d])

    def gb_recv(d, s):
        recv(gb_region(-s if d == 0 else s, s, d), bz_s.at[d, s - 1], bz_r.at[d, s - 1])

    def by_region(slot, yy):
        if slot >= 7:
            return wts.at[slot - 7, zat(4), yy, :, :, YS]
        off = -slot if slot < 4 else slot - 3
        return wts.at[:, zat(off), yy, :, :, YS]

    def gby_send(slot):
        r = by_region(slot, y)
        send(r, r, by_s.at[slot], by_r.at[slot], ydev)

    def gby_recv(slot):
        recv(by_region(slot, yo), by_s.at[slot], by_r.at[slot])

    got = (1 - nat) * 128
    give = nat * 128

    def forward(j):
        for a in range(2):
            rows = pl.ds(pl.multiple_of(768 + 256 * j + got, 128), 128)
            r = toks.at[a, rows, :]
            recv(r, tok_s.at[a, 0], tok_r.at[a, nat * j + (1 - nat) * (6 + j)])
            send(r, r, fwd_s.at[a, j], fwd_r.at[a, j], sib)

    def forwarded(j):
        for a in range(2):
            rows = pl.ds(pl.multiple_of(768 + 256 * j + give, 128), 128)
            recv(toks.at[a, rows, :], fwd_s.at[a, j], fwd_r.at[a, j])

    def own_tokens():
        @pl.when(is_nat)
        def _():
            for j in range(6):
                rows = pl.ds(128 * j, 128)
                pltpu.make_async_copy(cot.at[0, rows, :], toks.at[1, rows, :], load_s.at[1, j]).wait()

        @pl.when(jnp.logical_not(is_nat))
        def _():
            for j in range(6):
                for a in range(2):
                    recv(toks.at[a, pl.ds(128 * j, 128), :], tok_s.at[a, 0], tok_r.at[a, j])

    def values(first, count, offs):
        n = len(offs)

        def body(i, carry):
            k, group = i % 2, first + i // 2
            tk = pl.ds(pl.multiple_of(256 * group, 256), 256)
            lhs = jnp.concatenate([wts[k, zat(o)].reshape(64, DW) for o in offs], axis=0)
            out = lax.dot_general(lhs, toks[k, tk, :], (((1,), (1,)), ((), ())), preferred_element_type=F32)
            scale = jnp.where(k == 0, 1.0 / math.sqrt(DW), 1.0 / math.sqrt(HV)).astype(F32)
            out = (out * scale).astype(BF16)
            for b, o in enumerate(offs):
                vals[k, zat(o), :, :, :, tk] = out[64 * b:64 * b + 64].reshape(2, 2, 16, 256)
            return carry
        lax.fori_loop(0, 2 * count, body, 0)

    near, mid, far = (0, 1, 7), (2, 6), (3, 5, 4)

    r = wts.at[:, z, y, :, :, ZS]
    send(r, r, ay_s.at[0], ay_r.at[0], ydev)
    gb_send(0, 1)
    gb_send(1, 1)
    gby_send(0)
    normalize(1)
    normalize(4)
    recv(wts.at[:, z, yo, :, :, ZS], ay_s.at[0], ay_r.at[0])
    for k in range(2):
        ga_send(0, k, 1)
        ga_send(1, k, 1)
    normalize(2)
    normalize(5)

    def gather_step(s, work=()):
        work = list(work)

        def spare():
            if work:
                work.pop(0)()

        for d in range(2):
            gb_recv(d, s)
            if s < 4:
                gb_send(d, s + 1)
                gby_send(s + 3 * d)
            else:
                gby_send(7 + d)
            spare()
        for k in range(2):
            for d in range(2):
                if s < 4 or d == k:
                    ga_recv(d, k, s)
                    if s < 3 or (s == 3 and d == k):
                        ga_send(d, k, s + 1)
                    spare()
        for todo in work:
            todo()

    def value_work(first, count, offs):
        return lambda: values(first, count, offs)

    tokens_out((1, 4))
    gather_step(1)
    forward(0)
    tokens_out((2, 5))
    gather_step(2)
    own_tokens()
    for slot in (0, 1, 4):
        gby_recv(slot)
    gather_step(3, [value_work(g, 1, near) for g in range(3)])
    forward(1)
    forwarded(0)
    for slot in (2, 5):
        gby_recv(slot)
    gather_step(4, [value_work(3, 1, near)] + [value_work(g, 1, mid) for g in range(4)])
    for slot in (3, 6, 7, 8):
        gby_recv(slot)
    values(0, 4, far)
    forward(2)
    forwarded(1)
    values(4, 1, near + mid)
    values(4, 1, far)
    forwarded(2)
    values(5, 1, far)

    def grad_a(offs):
        def body(k, carry):
            lhs = jnp.concatenate([vals[1 - k, zat(o)].reshape(64, PAIR) for o in offs], axis=0)
            out = jnp.dot(lhs, toks[k, :, A0:B0], preferred_element_type=F32)
            for i, o in enumerate(offs):
                grad[k, zat(o), :, :, :, A0:B0] = out[64 * i:64 * i + 64].reshape(2, 2, 16, B0 - A0)
            return carry
        lax.fori_loop(0, 2, body, 0)

    def grad_b(yy):
        def body(k, carry):
            out = jnp.dot(vals[1 - k, :, yy].reshape(256, PAIR), toks[k, :, B0:C0], preferred_element_type=F32)
            grad[k, :, yy, :, :, B0:C0] = out.reshape(8, 2, 16, C0 - B0)
            return carry
        lax.fori_loop(0, 2, body, 0)

    def grad_c(xx):
        def body(k, carry):
            out = jnp.dot(vals[1 - k, :, :, xx].reshape(256, PAIR), toks[k, :, C0:DW], preferred_element_type=F32)
            grad[k, :, :, xx, :, C0:DW] = out.reshape(8, 2, 16, DW - C0)
            return carry
        lax.fori_loop(0, 2, body, 0)

    def rz_first(slot, d, k, s, off):
        sz[slot] = grad[k, zat(off), :, :, :, A0:B0].astype(BF16)
        send(sz.at[slot], rz.at[d, k, s - 1], cz_s.at[d, k, s - 1], cz_r.at[d, k, s - 1], zdev[d])

    def rz_hop(d, k, s):
        got = rz.at[d, k, s - 1]
        recv(got, cz_s.at[d, k, s - 1], cz_r.at[d, k, s - 1])
        off = 4 - s if d == 0 else s - 4
        rz[d, k, s - 1] = (rz[d, k, s - 1].astype(F32) + grad[k, zat(off), :, :, :, A0:B0]).astype(BF16)
        send(got, rz.at[d, k, s], cz_s.at[d, k, s], cz_r.at[d, k, s], zdev[d])

    xdev = (rep, fid(z, y, x + 2))

    def block(part, k, zz, own):
        if part == 0:
            return grad[k, zz, y if own else yo, :, :, B0:C0]
        return grad[k, zz, :, xh if own else 1 - xh, :, C0:DW]

    def half_send(part, i):
        for k in range(2):
            sy[part, i, k] = block(part, k, zat(ORDER[i]), False).astype(BF16)
        send(sy.at[part, i], ry.at[part, i], cy_s.at[part, i], cy_r.at[part, i], xdev if part else ydev)

    def half_recv(part, i):
        recv(ry.at[part, i], cy_s.at[part, i], cy_r.at[part, i])

    def r2_first(part):
        half_recv(part, 0)
        for k in range(2):
            ry[part, 0, k] = (ry[part, 0, k].astype(F32) + block(part, k, zat(4), True)).astype(BF16)
        for d in range(2):
            send(ry.at[part, 0, d], r2.at[part, d, 0, d], dz_s.at[part, d, 0], dz_r.at[part, d, 0], zdev[d])

    def r2_hop(part, d, s):
        off = (4 - s if d == 0 else s - 4) % Z
        i = ORDER.index(off)
        half_recv(part, i)
        if s == 1:
            recv(r2.at[part, d, 0, d], dz_s.at[part, d, 0], dz_r.at[part, d, 0])
        else:
            recv(r2.at[part, d, s - 1], dz_s.at[part, d, s - 1], dz_r.at[part, d, s - 1])
        for k in range(2):
            total = ry[part, i, k].astype(F32) + block(part, k, zat(off), True)
            if s > 1 or k == d:
                total = total + r2[part, d, s - 1, k].astype(F32)
            r2[part, d, s - 1, k] = total.astype(BF16)
        send(r2.at[part, d, s - 1], r2.at[part, d, s], dz_s.at[part, d, s], dz_r.at[part, d, s], zdev[d])

    def r2_last(part, k):
        return ((block(part, k, z, True) + ry[part, 7, k].astype(F32))
                + (r2[part, 0, 3, k].astype(F32) + r2[part, 1, 3, k].astype(F32)))

    def r2_end(part):
        half_recv(part, 7)
        for d in range(2):
            recv(r2.at[part, d, 3], dz_s.at[part, d, 3], dz_r.at[part, d, 3])

    cols = (pl.ds(A0, B0 - A0), pl.ds(B0, C0 - B0), pl.ds(C0, DW - C0))

    def owner_copies(part):
        out = []
        if part == 2:
            xo = 2 * c + xh
            out.append((fc, xs.at[0, :, :, cols[2]], 0, 0, xo))
        else:
            for xl in range(2):
                out.append((fx.at[xl, :, :, cols[part]], xs.at[xh, :, :, cols[part]], xl, xh, 2 * c + xl))
        return [o + (jnp.logical_and(o[4] == x, kx == c),) for o in out]

    def owner_send(part):
        for src, dst, i, j, xo, same in owner_copies(part):
            @pl.when(jnp.logical_not(same))
            def _(src=src, dst=dst, i=i, j=j, xo=xo):
                pltpu.make_async_remote_copy(src_ref=src, dst_ref=dst, send_sem=ex_s.at[part, i],
                                             recv_sem=ex_r.at[part, j], device_id=(2 * hi + kx, fid(z, y, xo)),
                                             device_id_type=MESH).start()

            @pl.when(same)
            def _(src=src, dst=dst, i=i):
                pltpu.make_async_copy(src, dst, ex_s.at[part, i]).start()

    def owner_wait(part):
        for d in range(1 if part == 2 else 2):
            region = xs.at[d, :, :, cols[part]]
            same = jnp.logical_and(is_nat, xh == c)
            if part < 2:
                same = jnp.logical_and(same, xh == d)

            @pl.when(jnp.logical_not(same))
            def _(region=region, d=d):
                recv(region, ex_s.at[part, 0], ex_r.at[part, d])
        for src, dst, i, j, xo, same in owner_copies(part):
            @pl.when(jnp.logical_not(same))
            def _(src=src, i=i):
                pltpu.make_async_remote_copy(src_ref=src, dst_ref=src, send_sem=ex_s.at[part, i],
                                             recv_sem=ex_r.at[part, 0], device_id=ydev,
                                             device_id_type=MESH).wait_send()

            @pl.when(same)
            def _(src=src, dst=dst, i=i):
                pltpu.make_async_copy(src, dst, ex_s.at[part, i]).wait()

    grad_a((4, 3, 5))
    rz_first(0, 0, 0, 1, 4)
    rz_first(1, 1, 1, 1, 4)
    rz_first(2, 0, 1, 2, 3)
    rz_first(3, 1, 0, 2, 5)
    values(5, 1, near + mid)
    grad_b(yo)
    for i in range(8):
        half_send(0, i)
    grad_c(1 - xh)
    for i in range(8):
        half_send(1, i)
    grad_a((2, 6, 1, 7, 0))
    rz_hop(0, 0, 1)
    rz_hop(1, 1, 1)
    grad_b(y)
    r2_first(0)
    rz_hop(0, 1, 2)
    rz_hop(1, 0, 2)
    grad_c(xh)
    r2_first(1)
    rz_hop(0, 0, 2)
    rz_hop(1, 1, 2)
    for part in range(2):
        r2_hop(part, 0, 1)
        r2_hop(part, 1, 1)
    rz_hop(0, 1, 3)
    rz_hop(1, 0, 3)
    rz_hop(0, 0, 3)
    rz_hop(1, 1, 3)
    for part in range(2):
        r2_hop(part, 0, 2)
        r2_hop(part, 1, 2)
    for d in range(2):
        for k in range(2):
            recv(rz.at[d, k, 3], cz_s.at[d, k, 3], cz_r.at[d, k, 3])
    for k in range(2):
        fs[k] = (grad[k, z, yo, :, :, A0:B0] + rz[0, k, 3, yo].astype(F32)) + rz[1, k, 3, yo].astype(F32)
    send(fs, fr, dy_s.at[0], dy_r.at[0], ydev)
    for k in range(2):
        mine = (grad[k, z, y, :, :, A0:B0] + rz[0, k, 3, y].astype(F32)) + rz[1, k, 3, y].astype(F32)
        for xl in range(2):
            fx[xl, k, :, A0:B0] = mine[xl]
    for part in range(2):
        r2_hop(part, 0, 3)
        r2_hop(part, 1, 3)
    recv(fr, dy_s.at[0], dy_r.at[0])
    for k in range(2):
        for xl in range(2):
            fx[xl, k, :, A0:B0] = fx[xl, k, :, A0:B0] + fr[k, xl]
    owner_send(0)
    r2_end(1)
    for k in range(2):
        mine = r2_last(1, k)
        sc[...] = mine
        gs[k] = sc[yo]
        fc[k] = sc[y]
    send(gs, gr, dy_s.at[1], dy_r.at[1], ydev)
    r2_end(0)
    for k in range(2):
        mine = r2_last(0, k)
        for xl in range(2):
            fx[xl, k, :, B0:C0] = mine[xl]
    owner_send(1)
    recv(gr, dy_s.at[1], dy_r.at[1])
    for k in range(2):
        fc[k] = fc[k] + gr[k]
    owner_send(2)
    for part in range(3):
        owner_wait(part)

    scale = inner_rate / math.sqrt(TOKENS)
    for k in range(2):
        inner_o[k, :, A0:C0] = params[0, :, k, A0:C0] - scale * (xs[0, k, :, A0:C0] + xs[1, k, :, A0:C0])
        inner_o[k, :, C0:DW] = params[0, :, k, C0:DW] - scale * xs[0, k, :, C0:DW]

    def fragment_of(array):
        pick = [array[:, FRAGW * i:FRAGW * (i + 1)] for i in range(NFRAG)]
        return jnp.where(index == 0, pick[0], jnp.where(index == 1, pick[1], pick[2]))

    for k in range(2):
        osend[k] = fragment_of(inner_o[k])
    for t, dev in enumerate(peers):
        send(osend, orecv.at[t], of_s.at[t], of_r.at[t], dev)
    for t in range(3):
        recv(moms.at[peers[t][0]], om_s.at[t], om_r.at[t])
    moms_o[...] = moms[...]
    for t in range(3):
        recv(orecv.at[t], of_s.at[t], of_r.at[t])
    for k in range(2):
        base = fragment_of(anchor[:, k, :])
        frag_o[k] = (((base - osend[k]) + (base - orecv[0, k])) + ((base - orecv[1, k]) + (base - orecv[2, k]))) * 0.25

    for d in range(2):
        xd = c + 2 * d
        same = jnp.logical_and(xd == x, xh == c)

        @pl.when(jnp.logical_not(same))
        def _(d=d):
            pltpu.make_async_remote_copy(src_ref=wown, dst_ref=wown, send_sem=wx_s.at[d], recv_sem=wx_r.at[0],
                                         device_id=ydev, device_id_type=MESH).wait_send()
    for cp in pending:
        cp.wait_send()


def window(inp, cot, params, anchor, moment, frag):
    dma = pltpu.SemaphoreType.DMA
    vmem = pltpu.VMEM
    both = lambda *shape: [dma(shape), dma(shape)]
    scratch = [
        vmem((2, PAIR, DW), BF16),
        vmem((TOK, DW), BF16),
        vmem((2, Z, Y, 2, ROWS, DW), BF16),
        vmem((2, ROWS, DW), BF16),
        vmem((2, Z, Y, 2, ROWS, PAIR), BF16),
        vmem((2, Z, Y, 2, ROWS, DW), F32),
        vmem((2, 2, 4, Y, 2, ROWS, B0 - A0), BF16),
        vmem((4, Y, 2, ROWS, B0 - A0), BF16),
        vmem((2, 8, 2, 2, ROWS, C0 - B0), BF16),
        vmem((2, 8, 2, 2, ROWS, C0 - B0), BF16),
        vmem((2, 2, 4, 2, 2, ROWS, C0 - B0), BF16),
        vmem((2, 2, ROWS, B0 - A0), F32),
        vmem((2, 2, ROWS, B0 - A0), F32),
        vmem((2, ROWS, DW - C0), F32),
        vmem((2, ROWS, DW - C0), F32),
        vmem((2, ROWS, DW - C0), F32),
        vmem((2, ROWS, DW - C0), F32),
        vmem((2, 2, ROWS, DW), F32),
        vmem((2, 2, ROWS, DW), F32),
        vmem((2, ROWS, FRAGW), F32),
        vmem((3, 2, ROWS, FRAGW), F32),
        vmem((4, 2, ROWS, QUARTER), F32),
        dma((2, 6)),
        dma((2, 6)), dma((2, 9)),
        *both(2, 3),
        *both(2),
        *both(1),
        *both(2, 2, 4),
        *both(2, 4),
        *both(9),
        *both(2, 2, 4),
        *both(2, 8),
        *both(2, 2, 4),
        *both(2),
        *both(3, 2),
        *both(3),
        *both(3),
    ]
    whole = pl.BlockSpec(memory_space=pltpu.VMEM)
    return pl.pallas_call(
        kernel,
        out_shape=(
            jax.ShapeDtypeStruct((2, ROWS, DW), F32),
            jax.ShapeDtypeStruct((2, ROWS, FRAGW), F32),
            jax.ShapeDtypeStruct((4, 2, ROWS, QUARTER), F32),
        ),
        in_specs=[pl.BlockSpec(memory_space=pl.ANY)] * 2 + [whole] * 3 + [pl.BlockSpec(memory_space=pltpu.SMEM)],
        out_specs=(whole, whole, whole),
        scratch_shapes=scratch,
        cost_estimate=pl.CostEstimate(flops=4 * 2 * TOK * DW * HV, bytes_accessed=10**7, transcendentals=TOK),
        compiler_params=pltpu.CompilerParams(
            collective_id=1, has_side_effects=True, vmem_limit_bytes=58 * 2**20
        ),
    )(inp, cot, params, anchor, moment, frag)


def finish(frag, inner, delta, moms, anchor, moment, replica_o, anchor_o, moment_o):
    index = frag[0]
    rep = lax.axis_index("rep")
    anchor_o[...] = anchor[...]
    moment_o[...] = moment[...]
    for k in range(2):
        change = delta[k]
        base = anchor[:, k, :]
        pick = [base[:, FRAGW * i:FRAGW * (i + 1)] for i in range(NFRAG)]
        base = jnp.where(index == 0, pick[0], jnp.where(index == 1, pick[1], pick[2]))
        old = jnp.concatenate([moms[r, k] for r in range(4)], axis=-1)
        new_moment = outer_momentum * old + change
        new_frag = base - outer_rate * (change + outer_momentum * new_moment)
        replica_o[0, :, k, :] = inner[k]
        for i in range(NFRAG):
            @pl.when(index == i)
            def _(i=i):
                replica_o[0, :, k, FRAGW * i:FRAGW * (i + 1)] = new_frag
                anchor_o[:, k, FRAGW * i:FRAGW * (i + 1)] = new_frag
        part = [new_moment[:, QUARTER * i:QUARTER * (i + 1)] for i in range(4)]
        low = jnp.where(rep == 0, part[0], part[1])
        high = jnp.where(rep == 2, part[2], part[3])
        moment_o[index, :, k, :] = jnp.where(rep < 2, low, high)


def per_device(inputs, cotangent, replica_params, anchor, momentum, fragment):
    inner, delta, moms = window(inputs, cotangent, replica_params, anchor, momentum, fragment)
    whole = pl.BlockSpec(memory_space=pltpu.VMEM)
    return pl.pallas_call(
        finish,
        out_shape=(
            jax.ShapeDtypeStruct((1, ROWS, 2, DW), F32),
            jax.ShapeDtypeStruct((ROWS, 2, DW), F32),
            jax.ShapeDtypeStruct((NFRAG, ROWS, 2, QUARTER), F32),
        ),
        in_specs=[pl.BlockSpec(memory_space=pltpu.SMEM)] + [whole] * 5,
        out_specs=(whole, whole, whole),
    )(fragment, inner, delta, moms, anchor, momentum)


def solution(mesh):
    return jax.shard_map(
        per_device,
        mesh=mesh,
        in_specs=(
            P("rep", "fsdp", None),
            P("rep", "fsdp", None),
            P("rep", "fsdp", None, None),
            P("fsdp", None, None),
            P(None, "fsdp", None, "rep"),
            P(),
        ),
        out_specs=(
            P("rep", "fsdp", None, None),
            P("fsdp", None, None),
            P(None, "fsdp", None, "rep"),
        ),
        check_vma=False,
    )
```

```python
import functools
import math

import jax
import jax.numpy as jnp
from jax import lax
from jax.experimental import pallas as pl
from jax.experimental.pallas import tpu as pltpu
from jax.sharding import PartitionSpec as P

DW = 2304
HV = 1024
NFRAG = 3
FRAGW = DW // NFRAG
QUARTER = FRAGW // 4
TOKENS = 49152
ROWS = 16
TOK = 768
PAIR = 2 * TOK
CZ = 896
CY = DW - CZ
A0, B0, C0 = 0, 512, 1408
Z, Y, X = 8, 2, 4

inner_rate = 0.5
outer_rate = 0.7
outer_momentum = 0.9
norm_epsilon = 1e-06

MESH = pl.DeviceIdType.MESH
F32 = jnp.float32
BF16 = jnp.bfloat16
ZS = pl.ds(0, CZ)
YS = pl.ds(CZ, CY)
ORDER = (4, 3, 5, 2, 6, 1, 7, 0)


def kernel(inp, cot, params_h, anchor_h, moment_h, frag, inner_o, frag_o, moms_o,
           toks, own, wts, wown, vals, grad, rz, sz, ry, sy, r2, fs, fr, fc, fx, xs, osend, orecv, moms, params, anchor, moment,
           small_s, load_s, tok_s, tok_r, fwd_s, fwd_r, wx_s, wx_r, ay_s, ay_r, az_s, az_r, bz_s, bz_r, by_s, by_r,
           cz_s, cz_r, cy_s, cy_r, dz_s, dz_r, dy_s, dy_r, ex_s, ex_r, om_s, om_r, of_s, of_r):
    rep = lax.axis_index("rep")
    f = lax.axis_index("fsdp")
    hi, c = rep // 2, rep % 2
    z, y, x = f // 8, (f // 4) % 2, f % 4
    kx, xh = x % 2, x // 2
    nat = 1 - (c + kx) % 2
    is_nat = nat == 1
    yo = 1 - y

    def fid(zz, yy, xx):
        return (zz % Z) * 8 + yy * 4 + xx % X

    def zat(offset):
        return (z + offset) % Z

    sib = (2 * hi + 1 - c, f)
    zdev = ((rep, fid(z + 1, y, x)), (rep, fid(z + 7, y, x)))
    ydev = (rep, fid(z, yo, x))
    peers = (sib, (2 * (1 - hi) + c, f), (2 * (1 - hi) + 1 - c, f))

    pending = []

    def send(src, dst, ssem, rsem, dev):
        cp = pltpu.make_async_remote_copy(src_ref=src, dst_ref=dst, send_sem=ssem, recv_sem=rsem,
                                          device_id=dev, device_id_type=MESH)
        cp.start()
        pending.append(cp)
        return cp

    def recv(region, ssem, rsem):
        pltpu.make_async_remote_copy(src_ref=region, dst_ref=region, send_sem=ssem, recv_sem=rsem,
                                     device_id=ydev, device_id_type=MESH).wait_recv()

    small = [pltpu.make_async_copy(a, b, small_s.at[i])
             for i, (a, b) in enumerate(((params_h, params), (moment_h, moment), (anchor_h, anchor)))]
    for cp in small:
        cp.start()
    barrier = pltpu.get_barrier_semaphore()
    group = [(2 * hi + (c + dc) % 2, fid(z, y, x + dx)) for dx in range(4) for dc in range(2) if dx or dc]
    group += [zdev[0], zdev[1], ydev, peers[1], peers[2]]
    group += [(2 * hi + kx, fid(z, yo, 2 * c + xh)), (2 * hi + xh, fid(z, yo, 2 * kx + c))]
    for dev in group:
        pl.semaphore_signal(barrier, inc=1, device_id=dev, device_id_type=MESH)

    loads = []
    for j in range(6):
        rows = pl.ds(128 * j, 128)
        cp = pltpu.make_async_copy(inp.at[0, rows, :], own.at[rows, :], load_s.at[0, j])
        cp.start()
        loads.append(cp)

    @pl.when(is_nat)
    def _():
        for j in range(6):
            rows = pl.ds(128 * j, 128)
            pltpu.make_async_copy(cot.at[0, rows, :], toks.at[1, rows, :], load_s.at[1, j]).start()

    index = frag[0]
    small[0].wait()
    small[1].wait()
    for k in range(2):
        wown[k] = params[0, :, k, :].astype(BF16)
        moms[rep, k] = moment[index, :, k, :]
    pl.semaphore_wait(barrier, len(group))

    for d in range(2):
        xd = c + 2 * d
        same = jnp.logical_and(xd == x, xh == c)
        dev = (2 * hi + xh, fid(z, y, xd))

        @pl.when(jnp.logical_not(same))
        def _(dev=dev, d=d):
            for i, cut in enumerate((YS, ZS)):
                pltpu.make_async_remote_copy(src_ref=wown.at[:, :, cut], dst_ref=wts.at[:, z, y, kx, :, cut],
                                             send_sem=wx_s.at[i, d], recv_sem=wx_r.at[i, kx],
                                             device_id=dev, device_id_type=MESH).start()

        @pl.when(same)
        def _(d=d):
            for i, cut in enumerate((YS, ZS)):
                pltpu.make_async_copy(wown.at[:, :, cut], wts.at[:, z, y, kx, :, cut], wx_s.at[i, d]).start()

    d0 = (nat * sib[0] + (1 - nat) * rep, fid(z, y, x + (1 - nat)))
    d1 = (sib[0], fid(z, y, x + 3 * (1 - nat)))

    def token_send(a, j):
        far = 768 + 256 * j if j < 3 else 768 + 256 * (j - 3) + 128
        rows = pl.ds(pl.multiple_of(nat * 128 * j + (1 - nat) * far, 128), 128)
        slot = j if j < 3 else j + 3 * (1 - nat)
        mine = pl.ds(128 * j, 128)
        src = own.at[mine, :] if a == 0 else cot.at[0, mine, :]
        send(src, toks.at[a, rows, :], tok_s.at[a, j], tok_r.at[a, slot], d0 if j < 3 else d1)

    def normalize(j):
        loads[j].wait()

        def body(i, carry):
            rows = pl.ds(pl.multiple_of(128 * j + 32 * i, 32), 32)
            wide = own[rows, :].astype(F32)
            out = (wide * lax.rsqrt(jnp.mean(wide * wide, axis=-1, keepdims=True) + norm_epsilon)).astype(BF16)
            own[rows, :] = out

            @pl.when(is_nat)
            def _():
                toks[0, rows, :] = out
            return carry
        lax.fori_loop(0, 4, body, 0)

    def tokens_out(js):
        for j in js:
            token_send(1, j)
            token_send(0, j)

    for j in (0, 3):
        normalize(j)
    for d in range(2):
        @pl.when(jnp.logical_not(jnp.logical_and(c + 2 * d == x, xh == c)))
        def _(d=d):
            for i, cut in enumerate((YS, ZS)):
                part = wown.at[:, :, cut]
                pltpu.make_async_remote_copy(src_ref=part, dst_ref=part, send_sem=wx_s.at[i, d], recv_sem=wx_r.at[i, 0],
                                             device_id=ydev, device_id_type=MESH).wait_send()
    tokens_out((0, 3))
    for t, dev in enumerate(peers):
        send(moms.at[rep], moms.at[rep], om_s.at[t], om_r.at[t], dev)

    def shards(i):
        cut = (YS, ZS)[i]
        for xl in range(2):
            here = wts.at[:, z, y, xl, :, cut]
            same = jnp.logical_and(jnp.logical_and(is_nat, xh == c), kx == xl)

            @pl.when(jnp.logical_not(same))
            def _(here=here, xl=xl):
                recv(here, wx_s.at[i, 0], wx_r.at[i, xl])

            @pl.when(same)
            def _(here=here):
                pltpu.make_async_copy(wown.at[:, :, cut], here, wx_s.at[i, xh]).wait()

    def ga_region(k, off):
        return wts.at[:, zat(off), yo if k else y, :, :, ZS]

    def ga_send(d, k, s):
        r = ga_region(k, -(s - 1) if d == 0 else s - 1)
        send(r, r, az_s.at[d, k, s - 1], az_r.at[d, k, s - 1], zdev[d])

    def ga_recv(d, k, s):
        recv(ga_region(k, -s if d == 0 else s), az_s.at[d, k, s - 1], az_r.at[d, k, s - 1])

    def gb_region(off, s, d):
        if s == 4:
            return wts.at[d, zat(off), y, :, :, YS]
        return wts.at[:, zat(off), y, :, :, YS]

    def gb_send(d, s):
        r = gb_region(-(s - 1) if d == 0 else s - 1, s, d)
        send(r, r, bz_s.at[d, s - 1], bz_r.at[d, s - 1], zdev[d])

    def gb_recv(d, s):
        recv(gb_region(-s if d == 0 else s, s, d), bz_s.at[d, s - 1], bz_r.at[d, s - 1])

    def by_region(slot, yy):
        if slot >= 7:
            return wts.at[slot - 7, zat(4), yy, :, :, YS]
        off = -slot if slot < 4 else slot - 3
        return wts.at[:, zat(off), yy, :, :, YS]

    def gby_send(slot):
        r = by_region(slot, y)
        send(r, r, by_s.at[slot], by_r.at[slot], ydev)

    def gby_recv(slot):
        recv(by_region(slot, yo), by_s.at[slot], by_r.at[slot])

    got = (1 - nat) * 128
    give = nat * 128

    def forward(j):
        for a in range(2):
            rows = pl.ds(pl.multiple_of(768 + 256 * j + got, 128), 128)
            r = toks.at[a, rows, :]
            recv(r, tok_s.at[a, 0], tok_r.at[a, nat * j + (1 - nat) * (6 + j)])
            send(r, r, fwd_s.at[a, j], fwd_r.at[a, j], sib)

    def forwarded(j):
        for a in range(2):
            rows = pl.ds(pl.multiple_of(768 + 256 * j + give, 128), 128)
            recv(toks.at[a, rows, :], fwd_s.at[a, j], fwd_r.at[a, j])

    def own_tokens():
        @pl.when(is_nat)
        def _():
            for j in range(6):
                rows = pl.ds(128 * j, 128)
                pltpu.make_async_copy(cot.at[0, rows, :], toks.at[1, rows, :], load_s.at[1, j]).wait()

        @pl.when(jnp.logical_not(is_nat))
        def _():
            for j in range(6):
                for a in range(2):
                    recv(toks.at[a, pl.ds(128 * j, 128), :], tok_s.at[a, 0], tok_r.at[a, j])

    def values(first, count, offs):
        n = len(offs)

        def body(i, carry):
            k, group = i % 2, first + i // 2
            tk = pl.ds(pl.multiple_of(256 * group, 256), 256)
            lhs = jnp.concatenate([wts[k, zat(o)].reshape(64, DW) for o in offs], axis=0)
            out = lax.dot_general(lhs, toks[k, tk, :], (((1,), (1,)), ((), ())), preferred_element_type=F32)
            scale = jnp.where(k == 0, 1.0 / math.sqrt(DW), 1.0 / math.sqrt(HV)).astype(F32)
            out = (out * scale).astype(BF16)
            for b, o in enumerate(offs):
                vals[k, zat(o), :, :, :, tk] = out[64 * b:64 * b + 64].reshape(2, 2, 16, 256)
            return carry
        lax.fori_loop(0, 2 * count, body, 0)

    def values_whole(group):
        def body(k, carry):
            tk = pl.ds(256 * group, 256)
            out = lax.dot_general(wts[k].reshape(512, DW), toks[k, tk, :], (((1,), (1,)), ((), ())),
                                  preferred_element_type=F32)
            scale = jnp.where(k == 0, 1.0 / math.sqrt(DW), 1.0 / math.sqrt(HV)).astype(F32)
            vals[k, :, :, :, :, tk] = (out * scale).astype(BF16).reshape(8, 2, 2, 16, 256)
            return carry
        lax.fori_loop(0, 2, body, 0)

    near, mid, far = (0, 1, 7), (2, 6), (3, 5, 4)

    shards(0)
    gb_send(0, 1)
    gb_send(1, 1)
    shards(1)
    r = wts.at[:, z, y, :, :, ZS]
    send(r, r, ay_s.at[0], ay_r.at[0], ydev)
    ga_send(0, 0, 1)
    ga_send(1, 0, 1)
    gby_send(0)
    normalize(1)
    normalize(4)
    recv(wts.at[:, z, yo, :, :, ZS], ay_s.at[0], ay_r.at[0])
    ga_send(0, 1, 1)
    ga_send(1, 1, 1)
    normalize(2)
    normalize(5)

    def gather_step(s, work=()):
        work = list(work)

        def spare():
            if work:
                work.pop(0)()

        for d in range(2):
            gb_recv(d, s)
            if s < 4:
                gb_send(d, s + 1)
                gby_send(s + 3 * d)
            else:
                gby_send(7 + d)
            spare()
        for k in range(2):
            for d in range(2):
                if s < 4 or d == k:
                    ga_recv(d, k, s)
                    if s < 3 or (s == 3 and d == k):
                        ga_send(d, k, s + 1)
                    spare()
        for todo in work:
            todo()

    def value_work(first, count, offs):
        return lambda: values(first, count, offs)

    tokens_out((1, 4))
    gather_step(1)
    forward(0)
    tokens_out((2, 5))
    gather_step(2)
    own_tokens()
    for slot in (0, 1, 4):
        gby_recv(slot)
    gather_step(3, [value_work(g, 1, near) for g in range(3)])
    forward(1)
    forwarded(0)
    for slot in (2, 5):
        gby_recv(slot)
    gather_step(4, [value_work(3, 1, near)] + [value_work(g, 1, mid) for g in range(4)])
    for slot in (3, 6, 7, 8):
        gby_recv(slot)
    values(0, 4, far)
    forward(2)
    forwarded(1)
    values_whole(4)
    forwarded(2)
    values_whole(5)

    def grad_a(offs):
        def body(k, carry):
            lhs = jnp.concatenate([vals[1 - k, zat(o)].reshape(64, PAIR) for o in offs], axis=0)
            out = jnp.dot(lhs, toks[k, :, A0:B0], preferred_element_type=F32)
            for i, o in enumerate(offs):
                grad[k, zat(o), :, :, :, A0:B0] = out[64 * i:64 * i + 64].reshape(2, 2, 16, B0 - A0)
            return carry
        lax.fori_loop(0, 2, body, 0)

    def grad_b(yy):
        def body(k, carry):
            out = jnp.dot(vals[1 - k, :, yy].reshape(256, PAIR), toks[k, :, B0:C0], preferred_element_type=F32)
            grad[k, :, yy, :, :, B0:C0] = out.reshape(8, 2, 16, C0 - B0)
            return carry
        lax.fori_loop(0, 2, body, 0)

    def grad_c(xx):
        def body(k, carry):
            out = jnp.dot(vals[1 - k, :, :, xx].reshape(256, PAIR), toks[k, :, C0:DW], preferred_element_type=F32)
            grad[k, :, :, xx, :, C0:DW] = out.reshape(8, 2, 16, DW - C0)
            return carry
        lax.fori_loop(0, 2, body, 0)

    def rz_first(slot, d, k, s, off):
        sz[slot] = grad[k, zat(off), :, :, :, A0:B0].astype(BF16)
        send(sz.at[slot], rz.at[d, k, s - 1], cz_s.at[d, k, s - 1], cz_r.at[d, k, s - 1], zdev[d])

    def rz_hop(d, k, s):
        got = rz.at[d, k, s - 1]
        recv(got, cz_s.at[d, k, s - 1], cz_r.at[d, k, s - 1])
        off = 4 - s if d == 0 else s - 4
        rz[d, k, s - 1] = (rz[d, k, s - 1].astype(F32) + grad[k, zat(off), :, :, :, A0:B0]).astype(BF16)
        send(got, rz.at[d, k, s], cz_s.at[d, k, s], cz_r.at[d, k, s], zdev[d])

    xdev = (rep, fid(z, y, x + 2))

    def block(part, k, zz, own):
        if part == 0:
            return grad[k, zz, y if own else yo, :, :, B0:C0]
        return grad[k, zz, :, xh if own else 1 - xh, :, C0:DW]

    def half_send(part, i):
        for k in range(2):
            sy[part, i, k] = block(part, k, zat(ORDER[i]), False).astype(BF16)
        send(sy.at[part, i], ry.at[part, i], cy_s.at[part, i], cy_r.at[part, i], xdev if part else ydev)

    def half_recv(part, i):
        recv(ry.at[part, i], cy_s.at[part, i], cy_r.at[part, i])

    def r2_first(part):
        half_recv(part, 0)
        for k in range(2):
            ry[part, 0, k] = (ry[part, 0, k].astype(F32) + block(part, k, zat(4), True)).astype(BF16)
        for d in range(2):
            send(ry.at[part, 0, d], r2.at[part, d, 0, d], dz_s.at[part, d, 0], dz_r.at[part, d, 0], zdev[d])

    def r2_hop(part, d, s):
        off = (4 - s if d == 0 else s - 4) % Z
        i = ORDER.index(off)
        half_recv(part, i)
        if s == 1:
            recv(r2.at[part, d, 0, d], dz_s.at[part, d, 0], dz_r.at[part, d, 0])
        else:
            recv(r2.at[part, d, s - 1], dz_s.at[part, d, s - 1], dz_r.at[part, d, s - 1])
        for k in range(2):
            total = ry[part, i, k].astype(F32) + block(part, k, zat(off), True)
            if s > 1 or k == d:
                total = total + r2[part, d, s - 1, k].astype(F32)
            r2[part, d, s - 1, k] = total.astype(BF16)
        send(r2.at[part, d, s - 1], r2.at[part, d, s], dz_s.at[part, d, s], dz_r.at[part, d, s], zdev[d])

    def r2_last(part, k):
        return ((block(part, k, z, True) + ry[part, 7, k].astype(F32))
                + (r2[part, 0, 3, k].astype(F32) + r2[part, 1, 3, k].astype(F32)))

    def r2_end(part):
        half_recv(part, 7)
        for d in range(2):
            recv(r2.at[part, d, 3], dz_s.at[part, d, 3], dz_r.at[part, d, 3])

    cols = (pl.ds(A0, B0 - A0), pl.ds(B0, C0 - B0), pl.ds(C0, DW - C0))

    def owner_copies(part):
        out = []
        if part == 2:
            for yy in range(2):
                out.append((fc.at[yy], xs.at[y, :, :, cols[2]], yy, y, yy, 2 * c + xh))
        else:
            for xl in range(2):
                out.append((fx.at[xl, :, :, cols[part]], xs.at[xh, :, :, cols[part]], xl, xh, y, 2 * c + xl))
        return [o + (jnp.logical_and(jnp.logical_and(o[5] == x, o[4] == y), kx == c),) for o in out]

    def owner_send(part):
        for src, dst, i, j, yt, xo, same in owner_copies(part):
            @pl.when(jnp.logical_not(same))
            def _(src=src, dst=dst, i=i, j=j, yt=yt, xo=xo):
                pltpu.make_async_remote_copy(src_ref=src, dst_ref=dst, send_sem=ex_s.at[part, i],
                                             recv_sem=ex_r.at[part, j], device_id=(2 * hi + kx, fid(z, yt, xo)),
                                             device_id_type=MESH).start()

            @pl.when(same)
            def _(src=src, dst=dst, i=i):
                pltpu.make_async_copy(src, dst, ex_s.at[part, i]).start()

    def owner_wait(part):
        for d in range(2):
            region = xs.at[d, :, :, cols[part]]
            same = jnp.logical_and(jnp.logical_and(is_nat, xh == c), (xh if part < 2 else y) == d)

            @pl.when(jnp.logical_not(same))
            def _(region=region, d=d):
                recv(region, ex_s.at[part, 0], ex_r.at[part, d])
        for src, dst, i, j, yt, xo, same in owner_copies(part):
            @pl.when(jnp.logical_not(same))
            def _(src=src, i=i):
                pltpu.make_async_remote_copy(src_ref=src, dst_ref=src, send_sem=ex_s.at[part, i],
                                             recv_sem=ex_r.at[part, 0], device_id=ydev,
                                             device_id_type=MESH).wait_send()

            @pl.when(same)
            def _(src=src, dst=dst, i=i):
                pltpu.make_async_copy(src, dst, ex_s.at[part, i]).wait()

    grad_a((4, 3, 5))
    rz_first(0, 0, 0, 1, 4)
    rz_first(1, 1, 1, 1, 4)
    rz_first(2, 0, 1, 2, 3)
    rz_first(3, 1, 0, 2, 5)
    grad_c(1 - xh)
    for i in range(8):
        half_send(1, i)
    grad_b(yo)
    for i in range(8):
        half_send(0, i)
    rz_hop(0, 0, 1)
    rz_hop(1, 1, 1)
    grad_a((2, 6, 1, 7, 0))
    rz_hop(0, 1, 2)
    rz_hop(1, 0, 2)
    grad_c(xh)
    r2_first(1)
    rz_hop(0, 0, 2)
    rz_hop(1, 1, 2)
    grad_b(y)
    r2_first(0)
    for part in (1, 0):
        r2_hop(part, 0, 1)
        r2_hop(part, 1, 1)
    rz_hop(0, 1, 3)
    rz_hop(1, 0, 3)
    rz_hop(0, 0, 3)
    rz_hop(1, 1, 3)
    for part in (1, 0):
        r2_hop(part, 0, 2)
        r2_hop(part, 1, 2)
    for d in range(2):
        for k in range(2):
            recv(rz.at[d, k, 3], cz_s.at[d, k, 3], cz_r.at[d, k, 3])
    for k in range(2):
        fs[k] = (grad[k, z, yo, :, :, A0:B0] + rz[0, k, 3, yo].astype(F32)) + rz[1, k, 3, yo].astype(F32)
    send(fs, fr, dy_s.at[0], dy_r.at[0], ydev)
    for k in range(2):
        mine = (grad[k, z, y, :, :, A0:B0] + rz[0, k, 3, y].astype(F32)) + rz[1, k, 3, y].astype(F32)
        for xl in range(2):
            fx[xl, k, :, A0:B0] = mine[xl]
    for part in (1, 0):
        r2_hop(part, 0, 3)
        r2_hop(part, 1, 3)
    recv(fr, dy_s.at[0], dy_r.at[0])
    for k in range(2):
        for xl in range(2):
            fx[xl, k, :, A0:B0] = fx[xl, k, :, A0:B0] + fr[k, xl]
    owner_send(0)
    r2_end(1)
    for k in range(2):
        mine = r2_last(1, k)
        for yy in range(2):
            fc[yy, k] = mine[yy]
    owner_send(2)
    r2_end(0)
    for k in range(2):
        mine = r2_last(0, k)
        for xl in range(2):
            fx[xl, k, :, B0:C0] = mine[xl]
    owner_send(1)
    for part in range(3):
        owner_wait(part)

    scale = inner_rate / math.sqrt(TOKENS)
    for k in range(2):
        inner_o[k] = params[0, :, k, :] - scale * (xs[0, k] + xs[1, k])

    def fragment_of(array):
        pick = [array[:, FRAGW * i:FRAGW * (i + 1)] for i in range(NFRAG)]
        return jnp.where(index == 0, pick[0], jnp.where(index == 1, pick[1], pick[2]))

    for k in range(2):
        osend[k] = fragment_of(inner_o[k])
    for t, dev in enumerate(peers):
        send(osend, orecv.at[t], of_s.at[t], of_r.at[t], dev)
    for t in range(3):
        recv(moms.at[peers[t][0]], om_s.at[t], om_r.at[t])
    moms_o[...] = moms[...]
    for t in range(3):
        recv(orecv.at[t], of_s.at[t], of_r.at[t])
    small[2].wait()
    for k in range(2):
        base = fragment_of(anchor[:, k, :])
        frag_o[k] = (((base - osend[k]) + (base - orecv[0, k])) + ((base - orecv[1, k]) + (base - orecv[2, k]))) * 0.25

    for cp in pending:
        cp.wait_send()


def window(inp, cot, params, anchor, moment, frag):
    dma = pltpu.SemaphoreType.DMA
    vmem = pltpu.VMEM
    both = lambda *shape: [dma(shape), dma(shape)]
    scratch = [
        vmem((2, PAIR, DW), BF16),
        vmem((TOK, DW), BF16),
        vmem((2, Z, Y, 2, ROWS, DW), BF16),
        vmem((2, ROWS, DW), BF16),
        vmem((2, Z, Y, 2, ROWS, PAIR), BF16),
        vmem((2, Z, Y, 2, ROWS, DW), F32),
        vmem((2, 2, 4, Y, 2, ROWS, B0 - A0), BF16),
        vmem((4, Y, 2, ROWS, B0 - A0), BF16),
        vmem((2, 8, 2, 2, ROWS, C0 - B0), BF16),
        vmem((2, 8, 2, 2, ROWS, C0 - B0), BF16),
        vmem((2, 2, 4, 2, 2, ROWS, C0 - B0), BF16),
        vmem((2, 2, ROWS, B0 - A0), F32),
        vmem((2, 2, ROWS, B0 - A0), F32),
        vmem((2, 2, ROWS, DW - C0), F32),
        vmem((2, 2, ROWS, DW), F32),
        vmem((2, 2, ROWS, DW), F32),
        vmem((2, ROWS, FRAGW), F32),
        vmem((3, 2, ROWS, FRAGW), F32),
        vmem((4, 2, ROWS, QUARTER), F32),
        vmem((1, ROWS, 2, DW), F32),
        vmem((ROWS, 2, DW), F32),
        vmem((NFRAG, ROWS, 2, QUARTER), F32),
        dma((3,)),
        dma((2, 6)),
        dma((2, 6)), dma((2, 9)),
        *both(2, 3),
        *both(2, 2),
        *both(1),
        *both(2, 2, 4),
        *both(2, 4),
        *both(9),
        *both(2, 2, 4),
        *both(2, 8),
        *both(2, 2, 4),
        *both(1),
        *both(3, 2),
        *both(3),
        *both(3),
    ]
    whole = pl.BlockSpec(memory_space=pltpu.VMEM)
    return pl.pallas_call(
        kernel,
        out_shape=(
            jax.ShapeDtypeStruct((2, ROWS, DW), F32),
            jax.ShapeDtypeStruct((2, ROWS, FRAGW), F32),
            jax.ShapeDtypeStruct((4, 2, ROWS, QUARTER), F32),
        ),
        in_specs=[pl.BlockSpec(memory_space=pl.ANY)] * 5 + [pl.BlockSpec(memory_space=pltpu.SMEM)],
        out_specs=(whole, whole, whole),
        scratch_shapes=scratch,
        cost_estimate=pl.CostEstimate(flops=4 * 2 * TOK * DW * HV, bytes_accessed=10**7, transcendentals=TOK),
        compiler_params=pltpu.CompilerParams(
            collective_id=1, has_side_effects=True, vmem_limit_bytes=58 * 2**20
        ),
    )(inp, cot, params, anchor, moment, frag)


def finish(frag, inner, delta, moms, anchor, moment, replica_o, anchor_o, moment_o):
    index = frag[0]
    rep = lax.axis_index("rep")
    anchor_o[...] = anchor[...]
    moment_o[...] = moment[...]
    for k in range(2):
        change = delta[k]
        base = anchor[:, k, :]
        pick = [base[:, FRAGW * i:FRAGW * (i + 1)] for i in range(NFRAG)]
        base = jnp.where(index == 0, pick[0], jnp.where(index == 1, pick[1], pick[2]))
        old = jnp.concatenate([moms[r, k] for r in range(4)], axis=-1)
        new_moment = outer_momentum * old + change
        new_frag = base - outer_rate * (change + outer_momentum * new_moment)
        replica_o[0, :, k, :] = inner[k]
        for i in range(NFRAG):
            @pl.when(index == i)
            def _(i=i):
                replica_o[0, :, k, FRAGW * i:FRAGW * (i + 1)] = new_frag
                anchor_o[:, k, FRAGW * i:FRAGW * (i + 1)] = new_frag
        part = [new_moment[:, QUARTER * i:QUARTER * (i + 1)] for i in range(4)]
        low = jnp.where(rep == 0, part[0], part[1])
        high = jnp.where(rep == 2, part[2], part[3])
        moment_o[index, :, k, :] = jnp.where(rep < 2, low, high)


def per_device(inputs, cotangent, replica_params, anchor, momentum, fragment):
    inner, delta, moms = window(inputs, cotangent, replica_params, anchor, momentum, fragment)
    whole = pl.BlockSpec(memory_space=pltpu.VMEM)
    return pl.pallas_call(
        finish,
        out_shape=(
            jax.ShapeDtypeStruct((1, ROWS, 2, DW), F32),
            jax.ShapeDtypeStruct((ROWS, 2, DW), F32),
            jax.ShapeDtypeStruct((NFRAG, ROWS, 2, QUARTER), F32),
        ),
        in_specs=[pl.BlockSpec(memory_space=pltpu.SMEM)] + [whole] * 5,
        out_specs=(whole, whole, whole),
    )(fragment, inner, delta, moms, anchor, momentum)


def solution(mesh):
    return jax.shard_map(
        per_device,
        mesh=mesh,
        in_specs=(
            P("rep", "fsdp", None),
            P("rep", "fsdp", None),
            P("rep", "fsdp", None, None),
            P("fsdp", None, None),
            P(None, "fsdp", None, "rep"),
            P(),
        ),
        out_specs=(
            P("rep", "fsdp", None, None),
            P("fsdp", None, None),
            P(None, "fsdp", None, "rep"),
        ),
        check_vma=False,
    )
```

```python
import functools
import math

import jax
import jax.numpy as jnp
from jax import lax
from jax.experimental import pallas as pl
from jax.experimental.pallas import tpu as pltpu
from jax.sharding import PartitionSpec as P

DW = 2304
HV = 1024
NFRAG = 3
FRAGW = DW // NFRAG
QUARTER = FRAGW // 4
TOKENS = 49152
ROWS = 16
TOK = 768
PAIR = 2 * TOK
CZ = 896
CY = DW - CZ
A0, B0, C0 = 0, 512, 1408
Z, Y, X = 8, 2, 4

inner_rate = 0.5
outer_rate = 0.7
outer_momentum = 0.9
norm_epsilon = 1e-06

MESH = pl.DeviceIdType.MESH
F32 = jnp.float32
BF16 = jnp.bfloat16
ZS = pl.ds(0, CZ)
YS = pl.ds(CZ, CY)
ORDER = (4, 3, 5, 2, 6, 1, 7, 0)


def kernel(inp, cot, params_h, anchor_h, moment_h, frag, inner_o, frag_o, moms_o,
           toks, own, wts, wown, vals, grad, rz, sz, ry, sy, r2, fs, fr, fc, fx, xs, osend, orecv, moms, params, anchor, moment,
           small_s, load_s, tok_s, tok_r, fwd_s, fwd_r, wx_s, wx_r, ay_s, ay_r, az_s, az_r, bz_s, bz_r, by_s, by_r,
           cz_s, cz_r, cy_s, cy_r, dz_s, dz_r, dy_s, dy_r, ex_s, ex_r, om_s, om_r, of_s, of_r):
    rep = lax.axis_index("rep")
    f = lax.axis_index("fsdp")
    hi, c = rep // 2, rep % 2
    z, y, x = f // 8, (f // 4) % 2, f % 4
    kx, xh = x % 2, x // 2
    nat = 1 - (c + kx) % 2
    is_nat = nat == 1
    yo = 1 - y

    def fid(zz, yy, xx):
        return (zz % Z) * 8 + yy * 4 + xx % X

    def zat(offset):
        return (z + offset) % Z

    sib = (2 * hi + 1 - c, f)
    zdev = ((rep, fid(z + 1, y, x)), (rep, fid(z + 7, y, x)))
    ydev = (rep, fid(z, yo, x))
    peers = (sib, (2 * (1 - hi) + c, f), (2 * (1 - hi) + 1 - c, f))

    pending = []

    def send(src, dst, ssem, rsem, dev):
        cp = pltpu.make_async_remote_copy(src_ref=src, dst_ref=dst, send_sem=ssem, recv_sem=rsem,
                                          device_id=dev, device_id_type=MESH)
        cp.start()
        pending.append(cp)
        return cp

    def recv(region, ssem, rsem):
        pltpu.make_async_remote_copy(src_ref=region, dst_ref=region, send_sem=ssem, recv_sem=rsem,
                                     device_id=ydev, device_id_type=MESH).wait_recv()

    small = [pltpu.make_async_copy(a, b, small_s.at[i])
             for i, (a, b) in enumerate(((params_h, params), (moment_h, moment), (anchor_h, anchor)))]
    for cp in small:
        cp.start()
    barrier = pltpu.get_barrier_semaphore()
    group = [(2 * hi + (c + dc) % 2, fid(z, y, x + dx)) for dx in range(4) for dc in range(2) if dx or dc]
    group += [zdev[0], zdev[1], ydev, peers[1], peers[2]]
    group += [(2 * hi + kx, fid(z, yo, 2 * c + xh)), (2 * hi + xh, fid(z, yo, 2 * kx + c))]
    for dev in group:
        pl.semaphore_signal(barrier, inc=1, device_id=dev, device_id_type=MESH)

    loads = []
    for j in range(6):
        rows = pl.ds(128 * j, 128)
        cp = pltpu.make_async_copy(inp.at[0, rows, :], own.at[rows, :], load_s.at[0, j])
        cp.start()
        loads.append(cp)

    @pl.when(is_nat)
    def _():
        for j in range(6):
            rows = pl.ds(128 * j, 128)
            pltpu.make_async_copy(cot.at[0, rows, :], toks.at[1, rows, :], load_s.at[1, j]).start()

    index = frag[0]
    small[0].wait()
    small[1].wait()
    for k in range(2):
        wown[k] = params[0, :, k, :].astype(BF16)
        moms[rep, k] = moment[index, :, k, :]
    pl.semaphore_wait(barrier, len(group))

    for d in range(2):
        xd = c + 2 * d
        same = jnp.logical_and(xd == x, xh == c)
        dev = (2 * hi + xh, fid(z, y, xd))

        @pl.when(jnp.logical_not(same))
        def _(dev=dev, d=d):
            for i, cut in enumerate((YS, ZS)):
                pltpu.make_async_remote_copy(src_ref=wown.at[:, :, cut], dst_ref=wts.at[:, z, y, kx, :, cut],
                                             send_sem=wx_s.at[i, d], recv_sem=wx_r.at[i, kx],
                                             device_id=dev, device_id_type=MESH).start()

        @pl.when(same)
        def _(d=d):
            for i, cut in enumerate((YS, ZS)):
                pltpu.make_async_copy(wown.at[:, :, cut], wts.at[:, z, y, kx, :, cut], wx_s.at[i, d]).start()

    d0 = (nat * sib[0] + (1 - nat) * rep, fid(z, y, x + (1 - nat)))
    d1 = (sib[0], fid(z, y, x + 3 * (1 - nat)))

    def token_send(a, j):
        far = 768 + 256 * j if j < 3 else 768 + 256 * (j - 3) + 128
        rows = pl.ds(pl.multiple_of(nat * 128 * j + (1 - nat) * far, 128), 128)
        slot = j if j < 3 else j + 3 * (1 - nat)
        mine = pl.ds(128 * j, 128)
        src = own.at[mine, :] if a == 0 else cot.at[0, mine, :]
        send(src, toks.at[a, rows, :], tok_s.at[a, j], tok_r.at[a, slot], d0 if j < 3 else d1)

    def normalize(j):
        loads[j].wait()

        def body(i, carry):
            rows = pl.ds(pl.multiple_of(128 * j + 32 * i, 32), 32)
            wide = own[rows, :].astype(F32)
            out = (wide * lax.rsqrt(jnp.mean(wide * wide, axis=-1, keepdims=True) + norm_epsilon)).astype(BF16)
            own[rows, :] = out

            @pl.when(is_nat)
            def _():
                toks[0, rows, :] = out
            return carry
        lax.fori_loop(0, 4, body, 0)

    def tokens_out(js):
        for j in js:
            token_send(1, j)
            token_send(0, j)

    for j in (0, 3):
        normalize(j)
    for d in range(2):
        @pl.when(jnp.logical_not(jnp.logical_and(c + 2 * d == x, xh == c)))
        def _(d=d):
            for i, cut in enumerate((YS, ZS)):
                part = wown.at[:, :, cut]
                pltpu.make_async_remote_copy(src_ref=part, dst_ref=part, send_sem=wx_s.at[i, d], recv_sem=wx_r.at[i, 0],
                                             device_id=ydev, device_id_type=MESH).wait_send()
    tokens_out((0, 3))
    for t, dev in enumerate(peers):
        send(moms.at[rep], moms.at[rep], om_s.at[t], om_r.at[t], dev)

    def shards(i):
        cut = (YS, ZS)[i]
        for xl in range(2):
            here = wts.at[:, z, y, xl, :, cut]
            same = jnp.logical_and(jnp.logical_and(is_nat, xh == c), kx == xl)

            @pl.when(jnp.logical_not(same))
            def _(here=here, xl=xl):
                recv(here, wx_s.at[i, 0], wx_r.at[i, xl])

            @pl.when(same)
            def _(here=here):
                pltpu.make_async_copy(wown.at[:, :, cut], here, wx_s.at[i, xh]).wait()

    def ga_region(k, off):
        return wts.at[:, zat(off), yo if k else y, :, :, ZS]

    def ga_send(d, k, s):
        r = ga_region(k, -(s - 1) if d == 0 else s - 1)
        send(r, r, az_s.at[d, k, s - 1], az_r.at[d, k, s - 1], zdev[d])

    def ga_recv(d, k, s):
        recv(ga_region(k, -s if d == 0 else s), az_s.at[d, k, s - 1], az_r.at[d, k, s - 1])

    def gb_region(off, s, d):
        if s == 4:
            return wts.at[d, zat(off), y, :, :, YS]
        return wts.at[:, zat(off), y, :, :, YS]

    def gb_send(d, s):
        r = gb_region(-(s - 1) if d == 0 else s - 1, s, d)
        send(r, r, bz_s.at[d, s - 1], bz_r.at[d, s - 1], zdev[d])

    def gb_recv(d, s):
        recv(gb_region(-s if d == 0 else s, s, d), bz_s.at[d, s - 1], bz_r.at[d, s - 1])

    def by_region(slot, yy):
        if slot >= 7:
            return wts.at[slot - 7, zat(4), yy, :, :, YS]
        off = -slot if slot < 4 else slot - 3
        return wts.at[:, zat(off), yy, :, :, YS]

    def gby_send(slot):
        r = by_region(slot, y)
        send(r, r, by_s.at[slot], by_r.at[slot], ydev)

    def gby_recv(slot):
        recv(by_region(slot, yo), by_s.at[slot], by_r.at[slot])

    got = (1 - nat) * 128
    give = nat * 128

    def forward(j):
        for a in range(2):
            rows = pl.ds(pl.multiple_of(768 + 256 * j + got, 128), 128)
            r = toks.at[a, rows, :]
            recv(r, tok_s.at[a, 0], tok_r.at[a, nat * j + (1 - nat) * (6 + j)])
            send(r, r, fwd_s.at[a, j], fwd_r.at[a, j], sib)

    def forwarded(j):
        for a in range(2):
            rows = pl.ds(pl.multiple_of(768 + 256 * j + give, 128), 128)
            recv(toks.at[a, rows, :], fwd_s.at[a, j], fwd_r.at[a, j])

    def own_tokens():
        @pl.when(is_nat)
        def _():
            for j in range(6):
                rows = pl.ds(128 * j, 128)
                pltpu.make_async_copy(cot.at[0, rows, :], toks.at[1, rows, :], load_s.at[1, j]).wait()

        @pl.when(jnp.logical_not(is_nat))
        def _():
            for j in range(6):
                for a in range(2):
                    recv(toks.at[a, pl.ds(128 * j, 128), :], tok_s.at[a, 0], tok_r.at[a, j])

    def values(first, count, offs):
        n = len(offs)

        def body(i, carry):
            k, group = i % 2, first + i // 2
            tk = pl.ds(pl.multiple_of(256 * group, 256), 256)
            lhs = jnp.concatenate([wts[k, zat(o)].reshape(64, DW) for o in offs], axis=0)
            out = lax.dot_general(lhs, toks[k, tk, :], (((1,), (1,)), ((), ())), preferred_element_type=F32)
            scale = jnp.where(k == 0, 1.0 / math.sqrt(DW), 1.0 / math.sqrt(HV)).astype(F32)
            out = (out * scale).astype(BF16)
            for b, o in enumerate(offs):
                vals[k, zat(o), :, :, :, tk] = out[64 * b:64 * b + 64].reshape(2, 2, 16, 256)
            return carry
        lax.fori_loop(0, 2 * count, body, 0)

    def values_whole(group):
        def body(k, carry):
            tk = pl.ds(256 * group, 256)
            out = lax.dot_general(wts[k].reshape(512, DW), toks[k, tk, :], (((1,), (1,)), ((), ())),
                                  preferred_element_type=F32)
            scale = jnp.where(k == 0, 1.0 / math.sqrt(DW), 1.0 / math.sqrt(HV)).astype(F32)
            vals[k, :, :, :, :, tk] = (out * scale).astype(BF16).reshape(8, 2, 2, 16, 256)
            return carry
        lax.fori_loop(0, 2, body, 0)

    near, mid, far = (0, 1, 7), (2, 6), (3, 5, 4)

    shards(0)
    gb_send(0, 1)
    gb_send(1, 1)
    shards(1)
    r = wts.at[:, z, y, :, :, ZS]
    send(r, r, ay_s.at[0], ay_r.at[0], ydev)
    ga_send(0, 0, 1)
    ga_send(1, 0, 1)
    gby_send(0)
    normalize(1)
    normalize(4)
    recv(wts.at[:, z, yo, :, :, ZS], ay_s.at[0], ay_r.at[0])
    ga_send(0, 1, 1)
    ga_send(1, 1, 1)
    normalize(2)
    normalize(5)

    def gather_step(s, work=()):
        work = list(work)

        def spare():
            if work:
                work.pop(0)()

        for d in range(2):
            gb_recv(d, s)
            if s < 4:
                gb_send(d, s + 1)
                gby_send(s + 3 * d)
            else:
                gby_send(7 + d)
            spare()
        for k in range(2):
            for d in range(2):
                if s < 4 or d == k:
                    ga_recv(d, k, s)
                    if s < 3 or (s == 3 and d == k):
                        ga_send(d, k, s + 1)
                    spare()
        for todo in work:
            todo()

    def value_work(first, count, offs):
        return lambda: values(first, count, offs)

    tokens_out((1, 4))
    gather_step(1)
    forward(0)
    tokens_out((2, 5))
    gather_step(2)
    own_tokens()
    for slot in (0, 1, 4):
        gby_recv(slot)
    gather_step(3)
    forward(1)
    forwarded(0)
    for slot in (2, 5):
        gby_recv(slot)
    gather_step(4, [value_work(g, 1, near + mid) for g in range(4)])
    for slot in (3, 6, 7, 8):
        gby_recv(slot)
    values(0, 4, far)
    forward(2)
    forwarded(1)
    values_whole(4)
    forwarded(2)
    values_whole(5)

    def grad_a(offs):
        def body(k, carry):
            lhs = jnp.concatenate([vals[1 - k, zat(o)].reshape(64, PAIR) for o in offs], axis=0)
            out = jnp.dot(lhs, toks[k, :, A0:B0], preferred_element_type=F32)
            for i, o in enumerate(offs):
                grad[k, zat(o), :, :, :, A0:B0] = out[64 * i:64 * i + 64].reshape(2, 2, 16, B0 - A0)
            return carry
        lax.fori_loop(0, 2, body, 0)

    def grad_b(yy):
        def body(k, carry):
            out = jnp.dot(vals[1 - k, :, yy].reshape(256, PAIR), toks[k, :, B0:C0], preferred_element_type=F32)
            grad[k, :, yy, :, :, B0:C0] = out.reshape(8, 2, 16, C0 - B0)
            return carry
        lax.fori_loop(0, 2, body, 0)

    def grad_c(xx):
        def body(k, carry):
            out = jnp.dot(vals[1 - k, :, :, xx].reshape(256, PAIR), toks[k, :, C0:DW], preferred_element_type=F32)
            grad[k, :, :, xx, :, C0:DW] = out.reshape(8, 2, 16, DW - C0)
            return carry
        lax.fori_loop(0, 2, body, 0)

    def rz_first(slot, d, k, s, off):
        sz[slot] = grad[k, zat(off), :, :, :, A0:B0].astype(BF16)
        send(sz.at[slot], rz.at[d, k, s - 1], cz_s.at[d, k, s - 1], cz_r.at[d, k, s - 1], zdev[d])

    def rz_hop(d, k, s):
        got = rz.at[d, k, s - 1]
        recv(got, cz_s.at[d, k, s - 1], cz_r.at[d, k, s - 1])
        off = 4 - s if d == 0 else s - 4
        rz[d, k, s - 1] = (rz[d, k, s - 1].astype(F32) + grad[k, zat(off), :, :, :, A0:B0]).astype(BF16)
        send(got, rz.at[d, k, s], cz_s.at[d, k, s], cz_r.at[d, k, s], zdev[d])

    xdev = (rep, fid(z, y, x + 2))

    def block(part, k, zz, own):
        if part == 0:
            return grad[k, zz, y if own else yo, :, :, B0:C0]
        return grad[k, zz, :, xh if own else 1 - xh, :, C0:DW]

    def half_send(part, i):
        for k in range(2):
            sy[part, i, k] = block(part, k, zat(ORDER[i]), False).astype(BF16)
        send(sy.at[part, i], ry.at[part, i], cy_s.at[part, i], cy_r.at[part, i], xdev if part else ydev)

    def half_recv(part, i):
        recv(ry.at[part, i], cy_s.at[part, i], cy_r.at[part, i])

    def r2_first(part):
        half_recv(part, 0)
        for k in range(2):
            ry[part, 0, k] = (ry[part, 0, k].astype(F32) + block(part, k, zat(4), True)).astype(BF16)
        for d in range(2):
            send(ry.at[part, 0, d], r2.at[part, d, 0, d], dz_s.at[part, d, 0], dz_r.at[part, d, 0], zdev[d])

    def r2_hop(part, d, s):
        off = (4 - s if d == 0 else s - 4) % Z
        i = ORDER.index(off)
        half_recv(part, i)
        if s == 1:
            recv(r2.at[part, d, 0, d], dz_s.at[part, d, 0], dz_r.at[part, d, 0])
        else:
            recv(r2.at[part, d, s - 1], dz_s.at[part, d, s - 1], dz_r.at[part, d, s - 1])
        for k in range(2):
            total = ry[part, i, k].astype(F32) + block(part, k, zat(off), True)
            if s > 1 or k == d:
                total = total + r2[part, d, s - 1, k].astype(F32)
            r2[part, d, s - 1, k] = total.astype(BF16)
        send(r2.at[part, d, s - 1], r2.at[part, d, s], dz_s.at[part, d, s], dz_r.at[part, d, s], zdev[d])

    def r2_last(part, k):
        return ((block(part, k, z, True) + ry[part, 7, k].astype(F32))
                + (r2[part, 0, 3, k].astype(F32) + r2[part, 1, 3, k].astype(F32)))

    def r2_end(part):
        half_recv(part, 7)
        for d in range(2):
            recv(r2.at[part, d, 3], dz_s.at[part, d, 3], dz_r.at[part, d, 3])

    cols = (pl.ds(A0, B0 - A0), pl.ds(B0, C0 - B0), pl.ds(C0, DW - C0))

    def owner_copies(part):
        out = []
        if part == 2:
            for yy in range(2):
                out.append((fc.at[yy], xs.at[y, :, :, cols[2]], yy, y, yy, 2 * c + xh))
        else:
            for xl in range(2):
                out.append((fx.at[xl, :, :, cols[part]], xs.at[xh, :, :, cols[part]], xl, xh, y, 2 * c + xl))
        return [o + (jnp.logical_and(jnp.logical_and(o[5] == x, o[4] == y), kx == c),) for o in out]

    def owner_send(part):
        for src, dst, i, j, yt, xo, same in owner_copies(part):
            @pl.when(jnp.logical_not(same))
            def _(src=src, dst=dst, i=i, j=j, yt=yt, xo=xo):
                pltpu.make_async_remote_copy(src_ref=src, dst_ref=dst, send_sem=ex_s.at[part, i],
                                             recv_sem=ex_r.at[part, j], device_id=(2 * hi + kx, fid(z, yt, xo)),
                                             device_id_type=MESH).start()

            @pl.when(same)
            def _(src=src, dst=dst, i=i):
                pltpu.make_async_copy(src, dst, ex_s.at[part, i]).start()

    def owner_wait(part):
        for d in range(2):
            region = xs.at[d, :, :, cols[part]]
            same = jnp.logical_and(jnp.logical_and(is_nat, xh == c), (xh if part < 2 else y) == d)

            @pl.when(jnp.logical_not(same))
            def _(region=region, d=d):
                recv(region, ex_s.at[part, 0], ex_r.at[part, d])
        for src, dst, i, j, yt, xo, same in owner_copies(part):
            @pl.when(jnp.logical_not(same))
            def _(src=src, i=i):
                pltpu.make_async_remote_copy(src_ref=src, dst_ref=src, send_sem=ex_s.at[part, i],
                                             recv_sem=ex_r.at[part, 0], device_id=ydev,
                                             device_id_type=MESH).wait_send()

            @pl.when(same)
            def _(src=src, dst=dst, i=i):
                pltpu.make_async_copy(src, dst, ex_s.at[part, i]).wait()

    grad_a((4, 3, 5))
    rz_first(0, 0, 0, 1, 4)
    rz_first(1, 1, 1, 1, 4)
    rz_first(2, 0, 1, 2, 3)
    rz_first(3, 1, 0, 2, 5)
    grad_c(1 - xh)
    for i in range(8):
        half_send(1, i)
    grad_b(yo)
    for i in range(8):
        half_send(0, i)
    rz_hop(0, 0, 1)
    rz_hop(1, 1, 1)
    grad_a((2, 6, 1, 7, 0))
    rz_hop(0, 1, 2)
    rz_hop(1, 0, 2)
    grad_c(xh)
    r2_first(1)
    rz_hop(0, 0, 2)
    rz_hop(1, 1, 2)
    grad_b(y)
    r2_first(0)
    for part in (1, 0):
        r2_hop(part, 0, 1)
        r2_hop(part, 1, 1)
    rz_hop(0, 1, 3)
    rz_hop(1, 0, 3)
    rz_hop(0, 0, 3)
    rz_hop(1, 1, 3)
    for part in (1, 0):
        r2_hop(part, 0, 2)
        r2_hop(part, 1, 2)
    for d in range(2):
        for k in range(2):
            recv(rz.at[d, k, 3], cz_s.at[d, k, 3], cz_r.at[d, k, 3])
    for k in range(2):
        fs[k] = (grad[k, z, yo, :, :, A0:B0] + rz[0, k, 3, yo].astype(F32)) + rz[1, k, 3, yo].astype(F32)
    send(fs, fr, dy_s.at[0], dy_r.at[0], ydev)
    for k in range(2):
        mine = (grad[k, z, y, :, :, A0:B0] + rz[0, k, 3, y].astype(F32)) + rz[1, k, 3, y].astype(F32)
        for xl in range(2):
            fx[xl, k, :, A0:B0] = mine[xl]
    for part in (1, 0):
        r2_hop(part, 0, 3)
        r2_hop(part, 1, 3)
    recv(fr, dy_s.at[0], dy_r.at[0])
    for k in range(2):
        for xl in range(2):
            fx[xl, k, :, A0:B0] = fx[xl, k, :, A0:B0] + fr[k, xl]
    owner_send(0)
    r2_end(1)
    for k in range(2):
        mine = r2_last(1, k)
        for yy in range(2):
            fc[yy, k] = mine[yy]
    owner_send(2)
    r2_end(0)
    for k in range(2):
        mine = r2_last(0, k)
        for xl in range(2):
            fx[xl, k, :, B0:C0] = mine[xl]
    owner_send(1)
    for part in range(3):
        owner_wait(part)

    scale = inner_rate / math.sqrt(TOKENS)
    for k in range(2):
        inner_o[k] = params[0, :, k, :] - scale * (xs[0, k] + xs[1, k])

    def fragment_of(array):
        pick = [array[:, FRAGW * i:FRAGW * (i + 1)] for i in range(NFRAG)]
        return jnp.where(index == 0, pick[0], jnp.where(index == 1, pick[1], pick[2]))

    for k in range(2):
        osend[k] = fragment_of(inner_o[k])
    for t, dev in enumerate(peers):
        send(osend, orecv.at[t], of_s.at[t], of_r.at[t], dev)
    for t in range(3):
        recv(moms.at[peers[t][0]], om_s.at[t], om_r.at[t])
    moms_o[...] = moms[...]
    for t in range(3):
        recv(orecv.at[t], of_s.at[t], of_r.at[t])
    small[2].wait()
    for k in range(2):
        base = fragment_of(anchor[:, k, :])
        frag_o[k] = (((base - osend[k]) + (base - orecv[0, k])) + ((base - orecv[1, k]) + (base - orecv[2, k]))) * 0.25

    for cp in pending:
        cp.wait_send()


def window(inp, cot, params, anchor, moment, frag):
    dma = pltpu.SemaphoreType.DMA
    vmem = pltpu.VMEM
    both = lambda *shape: [dma(shape), dma(shape)]
    scratch = [
        vmem((2, PAIR, DW), BF16),
        vmem((TOK, DW), BF16),
        vmem((2, Z, Y, 2, ROWS, DW), BF16),
        vmem((2, ROWS, DW), BF16),
        vmem((2, Z, Y, 2, ROWS, PAIR), BF16),
        vmem((2, Z, Y, 2, ROWS, DW), F32),
        vmem((2, 2, 4, Y, 2, ROWS, B0 - A0), BF16),
        vmem((4, Y, 2, ROWS, B0 - A0), BF16),
        vmem((2, 8, 2, 2, ROWS, C0 - B0), BF16),
        vmem((2, 8, 2, 2, ROWS, C0 - B0), BF16),
        vmem((2, 2, 4, 2, 2, ROWS, C0 - B0), BF16),
        vmem((2, 2, ROWS, B0 - A0), F32),
        vmem((2, 2, ROWS, B0 - A0), F32),
        vmem((2, 2, ROWS, DW - C0), F32),
        vmem((2, 2, ROWS, DW), F32),
        vmem((2, 2, ROWS, DW), F32),
        vmem((2, ROWS, FRAGW), F32),
        vmem((3, 2, ROWS, FRAGW), F32),
        vmem((4, 2, ROWS, QUARTER), F32),
        vmem((1, ROWS, 2, DW), F32),
        vmem((ROWS, 2, DW), F32),
        vmem((NFRAG, ROWS, 2, QUARTER), F32),
        dma((3,)),
        dma((2, 6)),
        dma((2, 6)), dma((2, 9)),
        *both(2, 3),
        *both(2, 2),
        *both(1),
        *both(2, 2, 4),
        *both(2, 4),
        *both(9),
        *both(2, 2, 4),
        *both(2, 8),
        *both(2, 2, 4),
        *both(1),
        *both(3, 2),
        *both(3),
        *both(3),
    ]
    whole = pl.BlockSpec(memory_space=pltpu.VMEM)
    return pl.pallas_call(
        kernel,
        out_shape=(
            jax.ShapeDtypeStruct((2, ROWS, DW), F32),
            jax.ShapeDtypeStruct((2, ROWS, FRAGW), F32),
            jax.ShapeDtypeStruct((4, 2, ROWS, QUARTER), F32),
        ),
        in_specs=[pl.BlockSpec(memory_space=pl.ANY)] * 5 + [pl.BlockSpec(memory_space=pltpu.SMEM)],
        out_specs=(whole, whole, whole),
        scratch_shapes=scratch,
        cost_estimate=pl.CostEstimate(flops=4 * 2 * TOK * DW * HV, bytes_accessed=10**7, transcendentals=TOK),
        compiler_params=pltpu.CompilerParams(
            collective_id=1, has_side_effects=True, vmem_limit_bytes=58 * 2**20
        ),
    )(inp, cot, params, anchor, moment, frag)


def finish(frag, inner, delta, moms, anchor, moment, replica_o, anchor_o, moment_o):
    index = frag[0]
    rep = lax.axis_index("rep")
    anchor_o[...] = anchor[...]
    moment_o[...] = moment[...]
    for k in range(2):
        change = delta[k]
        base = anchor[:, k, :]
        pick = [base[:, FRAGW * i:FRAGW * (i + 1)] for i in range(NFRAG)]
        base = jnp.where(index == 0, pick[0], jnp.where(index == 1, pick[1], pick[2]))
        old = jnp.concatenate([moms[r, k] for r in range(4)], axis=-1)
        new_moment = outer_momentum * old + change
        new_frag = base - outer_rate * (change + outer_momentum * new_moment)
        replica_o[0, :, k, :] = inner[k]
        for i in range(NFRAG):
            @pl.when(index == i)
            def _(i=i):
                replica_o[0, :, k, FRAGW * i:FRAGW * (i + 1)] = new_frag
                anchor_o[:, k, FRAGW * i:FRAGW * (i + 1)] = new_frag
        part = [new_moment[:, QUARTER * i:QUARTER * (i + 1)] for i in range(4)]
        low = jnp.where(rep == 0, part[0], part[1])
        high = jnp.where(rep == 2, part[2], part[3])
        moment_o[index, :, k, :] = jnp.where(rep < 2, low, high)


def per_device(inputs, cotangent, replica_params, anchor, momentum, fragment):
    inner, delta, moms = window(inputs, cotangent, replica_params, anchor, momentum, fragment)
    whole = pl.BlockSpec(memory_space=pltpu.VMEM)
    return pl.pallas_call(
        finish,
        out_shape=(
            jax.ShapeDtypeStruct((1, ROWS, 2, DW), F32),
            jax.ShapeDtypeStruct((ROWS, 2, DW), F32),
            jax.ShapeDtypeStruct((NFRAG, ROWS, 2, QUARTER), F32),
        ),
        in_specs=[pl.BlockSpec(memory_space=pltpu.SMEM)] + [whole] * 5,
        out_specs=(whole, whole, whole),
    )(fragment, inner, delta, moms, anchor, momentum)


def solution(mesh):
    return jax.shard_map(
        per_device,
        mesh=mesh,
        in_specs=(
            P("rep", "fsdp", None),
            P("rep", "fsdp", None),
            P("rep", "fsdp", None, None),
            P("fsdp", None, None),
            P(None, "fsdp", None, "rep"),
            P(),
        ),
        out_specs=(
            P("rep", "fsdp", None, None),
            P("fsdp", None, None),
            P(None, "fsdp", None, "rep"),
        ),
        check_vma=False,
    )
```

```python
import functools
import math

import jax
import jax.numpy as jnp
from jax import lax
from jax.experimental import pallas as pl
from jax.experimental.pallas import tpu as pltpu
from jax.sharding import PartitionSpec as P

DW = 2304
HV = 1024
NFRAG = 3
FRAGW = DW // NFRAG
QUARTER = FRAGW // 4
TOKENS = 49152
ROWS = 16
TOK = 768
PAIR = 2 * TOK
CZ = 896
CY = DW - CZ
A0, B0, C0 = 0, 512, 1408
Z, Y, X = 8, 2, 4

inner_rate = 0.5
outer_rate = 0.7
outer_momentum = 0.9
norm_epsilon = 1e-06

MESH = pl.DeviceIdType.MESH
F32 = jnp.float32
BF16 = jnp.bfloat16
ZS = pl.ds(0, CZ)
YS = pl.ds(CZ, CY)
ORDER = (4, 3, 5, 2, 6, 1, 7, 0)


def kernel(inp, cot, params_h, anchor_h, moment_h, frag, inner_o, frag_o, moms_o,
           toks, own, wts, wown, vals, grad, rz, sz, ry, sy, r2, fs, fr, fc, fx, xs, osend, orecv, moms, params, anchor, moment,
           small_s, load_s, tok_s, tok_r, fwd_s, fwd_r, wx_s, wx_r, ay_s, ay_r, az_s, az_r, bz_s, bz_r, by_s, by_r,
           cz_s, cz_r, cy_s, cy_r, dz_s, dz_r, dy_s, dy_r, ex_s, ex_r, om_s, om_r, of_s, of_r):
    rep = lax.axis_index("rep")
    f = lax.axis_index("fsdp")
    hi, c = rep // 2, rep % 2
    z, y, x = f // 8, (f // 4) % 2, f % 4
    kx, xh = x % 2, x // 2
    nat = 1 - (c + kx) % 2
    is_nat = nat == 1
    yo = 1 - y

    def fid(zz, yy, xx):
        return (zz % Z) * 8 + yy * 4 + xx % X

    def zat(offset):
        return (z + offset) % Z

    sib = (2 * hi + 1 - c, f)
    zdev = ((rep, fid(z + 1, y, x)), (rep, fid(z + 7, y, x)))
    ydev = (rep, fid(z, yo, x))
    peers = (sib, (2 * (1 - hi) + c, f), (2 * (1 - hi) + 1 - c, f))

    pending = []

    def send(src, dst, ssem, rsem, dev):
        cp = pltpu.make_async_remote_copy(src_ref=src, dst_ref=dst, send_sem=ssem, recv_sem=rsem,
                                          device_id=dev, device_id_type=MESH)
        cp.start()
        pending.append(cp)
        return cp

    def recv(region, ssem, rsem):
        pltpu.make_async_remote_copy(src_ref=region, dst_ref=region, send_sem=ssem, recv_sem=rsem,
                                     device_id=ydev, device_id_type=MESH).wait_recv()

    small = [pltpu.make_async_copy(a, b, small_s.at[i])
             for i, (a, b) in enumerate(((params_h, params), (moment_h, moment), (anchor_h, anchor)))]
    for cp in small:
        cp.start()
    barrier = pltpu.get_barrier_semaphore()
    group = [(2 * hi + (c + dc) % 2, fid(z, y, x + dx)) for dx in range(4) for dc in range(2) if dx or dc]
    group += [zdev[0], zdev[1], ydev, peers[1], peers[2]]
    group += [(2 * hi + kx, fid(z, yo, 2 * c + xh)), (2 * hi + xh, fid(z, yo, 2 * kx + c))]
    for dev in group:
        pl.semaphore_signal(barrier, inc=1, device_id=dev, device_id_type=MESH)

    loads = []
    for j in range(6):
        rows = pl.ds(128 * j, 128)
        cp = pltpu.make_async_copy(inp.at[0, rows, :], own.at[rows, :], load_s.at[0, j])
        cp.start()
        loads.append(cp)

    @pl.when(is_nat)
    def _():
        for j in range(6):
            rows = pl.ds(128 * j, 128)
            pltpu.make_async_copy(cot.at[0, rows, :], toks.at[1, rows, :], load_s.at[1, j]).start()

    index = frag[0]
    small[0].wait()
    small[1].wait()
    for k in range(2):
        wown[k] = params[0, :, k, :].astype(BF16)
        moms[rep, k] = moment[index, :, k, :]
    pl.semaphore_wait(barrier, len(group))

    for d in range(2):
        xd = c + 2 * d
        same = jnp.logical_and(xd == x, xh == c)
        dev = (2 * hi + xh, fid(z, y, xd))

        @pl.when(jnp.logical_not(same))
        def _(dev=dev, d=d):
            for i, cut in enumerate((YS, ZS)):
                pltpu.make_async_remote_copy(src_ref=wown.at[:, :, cut], dst_ref=wts.at[:, z, y, kx, :, cut],
                                             send_sem=wx_s.at[i, d], recv_sem=wx_r.at[i, kx],
                                             device_id=dev, device_id_type=MESH).start()

        @pl.when(same)
        def _(d=d):
            for i, cut in enumerate((YS, ZS)):
                pltpu.make_async_copy(wown.at[:, :, cut], wts.at[:, z, y, kx, :, cut], wx_s.at[i, d]).start()

    d0 = (nat * sib[0] + (1 - nat) * rep, fid(z, y, x + (1 - nat)))
    d1 = (sib[0], fid(z, y, x + 3 * (1 - nat)))

    def token_send(a, j):
        far = 768 + 256 * j if j < 3 else 768 + 256 * (j - 3) + 128
        rows = pl.ds(pl.multiple_of(nat * 128 * j + (1 - nat) * far, 128), 128)
        slot = j if j < 3 else j + 3 * (1 - nat)
        mine = pl.ds(128 * j, 128)
        src = own.at[mine, :] if a == 0 else cot.at[0, mine, :]
        send(src, toks.at[a, rows, :], tok_s.at[a, j], tok_r.at[a, slot], d0 if j < 3 else d1)

    def normalize(j):
        loads[j].wait()

        def body(i, carry):
            rows = pl.ds(pl.multiple_of(128 * j + 32 * i, 32), 32)
            wide = own[rows, :].astype(F32)
            out = (wide * lax.rsqrt(jnp.mean(wide * wide, axis=-1, keepdims=True) + norm_epsilon)).astype(BF16)
            own[rows, :] = out

            @pl.when(is_nat)
            def _():
                toks[0, rows, :] = out
            return carry
        lax.fori_loop(0, 4, body, 0)

    def tokens_out(js):
        for j in js:
            token_send(1, j)
            token_send(0, j)

    for j in (0, 3):
        normalize(j)
    for d in range(2):
        @pl.when(jnp.logical_not(jnp.logical_and(c + 2 * d == x, xh == c)))
        def _(d=d):
            for i, cut in enumerate((YS, ZS)):
                part = wown.at[:, :, cut]
                pltpu.make_async_remote_copy(src_ref=part, dst_ref=part, send_sem=wx_s.at[i, d], recv_sem=wx_r.at[i, 0],
                                             device_id=ydev, device_id_type=MESH).wait_send()
    tokens_out((0, 3))
    for t, dev in enumerate(peers):
        send(moms.at[rep], moms.at[rep], om_s.at[t], om_r.at[t], dev)

    def shards(i):
        cut = (YS, ZS)[i]
        for xl in range(2):
            here = wts.at[:, z, y, xl, :, cut]
            same = jnp.logical_and(jnp.logical_and(is_nat, xh == c), kx == xl)

            @pl.when(jnp.logical_not(same))
            def _(here=here, xl=xl):
                recv(here, wx_s.at[i, 0], wx_r.at[i, xl])

            @pl.when(same)
            def _(here=here):
                pltpu.make_async_copy(wown.at[:, :, cut], here, wx_s.at[i, xh]).wait()

    def ga_region(k, off):
        return wts.at[:, zat(off), yo if k else y, :, :, ZS]

    def ga_send(d, k, s):
        r = ga_region(k, -(s - 1) if d == 0 else s - 1)
        send(r, r, az_s.at[d, k, s - 1], az_r.at[d, k, s - 1], zdev[d])

    def ga_recv(d, k, s):
        recv(ga_region(k, -s if d == 0 else s), az_s.at[d, k, s - 1], az_r.at[d, k, s - 1])

    def gb_region(off, s, d):
        if s == 4:
            return wts.at[d, zat(off), y, :, :, YS]
        return wts.at[:, zat(off), y, :, :, YS]

    def gb_send(d, s):
        r = gb_region(-(s - 1) if d == 0 else s - 1, s, d)
        send(r, r, bz_s.at[d, s - 1], bz_r.at[d, s - 1], zdev[d])

    def gb_recv(d, s):
        recv(gb_region(-s if d == 0 else s, s, d), bz_s.at[d, s - 1], bz_r.at[d, s - 1])

    def by_region(slot, yy):
        if slot >= 7:
            return wts.at[slot - 7, zat(4), yy, :, :, YS]
        off = -slot if slot < 4 else slot - 3
        return wts.at[:, zat(off), yy, :, :, YS]

    def gby_send(slot):
        r = by_region(slot, y)
        send(r, r, by_s.at[slot], by_r.at[slot], ydev)

    def gby_recv(slot):
        recv(by_region(slot, yo), by_s.at[slot], by_r.at[slot])

    got = (1 - nat) * 128
    give = nat * 128

    def forward(j):
        for a in range(2):
            rows = pl.ds(pl.multiple_of(768 + 256 * j + got, 128), 128)
            r = toks.at[a, rows, :]
            recv(r, tok_s.at[a, 0], tok_r.at[a, nat * j + (1 - nat) * (6 + j)])
            send(r, r, fwd_s.at[a, j], fwd_r.at[a, j], sib)

    def forwarded(j):
        for a in range(2):
            rows = pl.ds(pl.multiple_of(768 + 256 * j + give, 128), 128)
            recv(toks.at[a, rows, :], fwd_s.at[a, j], fwd_r.at[a, j])

    def own_tokens():
        @pl.when(is_nat)
        def _():
            for j in range(6):
                rows = pl.ds(128 * j, 128)
                pltpu.make_async_copy(cot.at[0, rows, :], toks.at[1, rows, :], load_s.at[1, j]).wait()

        @pl.when(jnp.logical_not(is_nat))
        def _():
            for j in range(6):
                for a in range(2):
                    recv(toks.at[a, pl.ds(128 * j, 128), :], tok_s.at[a, 0], tok_r.at[a, j])

    def values(first, count, offs):
        n = len(offs)

        def body(i, carry):
            k, group = i % 2, first + i // 2
            tk = pl.ds(pl.multiple_of(256 * group, 256), 256)
            lhs = jnp.concatenate([wts[k, zat(o)].reshape(64, DW) for o in offs], axis=0)
            out = lax.dot_general(lhs, toks[k, tk, :], (((1,), (1,)), ((), ())), preferred_element_type=F32)
            scale = jnp.where(k == 0, 1.0 / math.sqrt(DW), 1.0 / math.sqrt(HV)).astype(F32)
            out = (out * scale).astype(BF16)
            for b, o in enumerate(offs):
                vals[k, zat(o), :, :, :, tk] = out[64 * b:64 * b + 64].reshape(2, 2, 16, 256)
            return carry
        lax.fori_loop(0, 2 * count, body, 0)

    def values_whole(group):
        def body(k, carry):
            tk = pl.ds(256 * group, 256)
            out = lax.dot_general(wts[k].reshape(512, DW), toks[k, tk, :], (((1,), (1,)), ((), ())),
                                  preferred_element_type=F32)
            scale = jnp.where(k == 0, 1.0 / math.sqrt(DW), 1.0 / math.sqrt(HV)).astype(F32)
            vals[k, :, :, :, :, tk] = (out * scale).astype(BF16).reshape(8, 2, 2, 16, 256)
            return carry
        lax.fori_loop(0, 2, body, 0)

    near, mid, far = (0, 1, 7), (2, 6), (3, 5, 4)

    shards(0)
    gb_send(0, 1)
    gb_send(1, 1)
    shards(1)
    r = wts.at[:, z, y, :, :, ZS]
    send(r, r, ay_s.at[0], ay_r.at[0], ydev)
    ga_send(0, 0, 1)
    ga_send(1, 0, 1)
    gby_send(0)
    normalize(1)
    normalize(4)
    recv(wts.at[:, z, yo, :, :, ZS], ay_s.at[0], ay_r.at[0])
    ga_send(0, 1, 1)
    ga_send(1, 1, 1)
    normalize(2)
    normalize(5)

    def gather_step(s, work=()):
        work = list(work)

        def spare():
            if work:
                work.pop(0)()

        for d in range(2):
            gb_recv(d, s)
            if s < 4:
                gb_send(d, s + 1)
                gby_send(s + 3 * d)
            else:
                gby_send(7 + d)
            spare()
        for k in range(2):
            for d in range(2):
                if s < 4 or d == k:
                    ga_recv(d, k, s)
                    if s < 3 or (s == 3 and d == k):
                        ga_send(d, k, s + 1)
                    spare()
        for todo in work:
            todo()

    def value_work(first, count, offs):
        return lambda: values(first, count, offs)

    tokens_out((1, 4))
    gather_step(1)
    forward(0)
    tokens_out((2, 5))
    gather_step(2)
    own_tokens()
    for slot in (0, 1, 4):
        gby_recv(slot)
    gather_step(3)
    forward(1)
    forwarded(0)
    for slot in (2, 5):
        gby_recv(slot)
    gather_step(4, [value_work(g, 1, near + mid) for g in range(4)])
    for slot in (3, 6, 7, 8):
        gby_recv(slot)
    values(0, 2, far)
    forward(2)
    values(2, 2, far)
    forwarded(1)
    values_whole(4)
    forwarded(2)
    values_whole(5)

    def grad_a(offs):
        def body(k, carry):
            lhs = jnp.concatenate([vals[1 - k, zat(o)].reshape(64, PAIR) for o in offs], axis=0)
            out = jnp.dot(lhs, toks[k, :, A0:B0], preferred_element_type=F32)
            for i, o in enumerate(offs):
                grad[k, zat(o), :, :, :, A0:B0] = out[64 * i:64 * i + 64].reshape(2, 2, 16, B0 - A0)
            return carry
        lax.fori_loop(0, 2, body, 0)

    def grad_b(yy):
        def body(k, carry):
            out = jnp.dot(vals[1 - k, :, yy].reshape(256, PAIR), toks[k, :, B0:C0], preferred_element_type=F32)
            grad[k, :, yy, :, :, B0:C0] = out.reshape(8, 2, 16, C0 - B0)
            return carry
        lax.fori_loop(0, 2, body, 0)

    def grad_c(xx):
        def body(k, carry):
            out = jnp.dot(vals[1 - k, :, :, xx].reshape(256, PAIR), toks[k, :, C0:DW], preferred_element_type=F32)
            grad[k, :, :, xx, :, C0:DW] = out.reshape(8, 2, 16, DW - C0)
            return carry
        lax.fori_loop(0, 2, body, 0)

    def rz_first(slot, d, k, s, off):
        sz[slot] = grad[k, zat(off), :, :, :, A0:B0].astype(BF16)
        send(sz.at[slot], rz.at[d, k, s - 1], cz_s.at[d, k, s - 1], cz_r.at[d, k, s - 1], zdev[d])

    def rz_hop(d, k, s):
        got = rz.at[d, k, s - 1]
        recv(got, cz_s.at[d, k, s - 1], cz_r.at[d, k, s - 1])
        off = 4 - s if d == 0 else s - 4
        rz[d, k, s - 1] = (rz[d, k, s - 1].astype(F32) + grad[k, zat(off), :, :, :, A0:B0]).astype(BF16)
        send(got, rz.at[d, k, s], cz_s.at[d, k, s], cz_r.at[d, k, s], zdev[d])

    xdev = (rep, fid(z, y, x + 2))

    def block(part, k, zz, own):
        if part == 0:
            return grad[k, zz, y if own else yo, :, :, B0:C0]
        return grad[k, zz, :, xh if own else 1 - xh, :, C0:DW]

    def half_send(part, i):
        for k in range(2):
            sy[part, i, k] = block(part, k, zat(ORDER[i]), False).astype(BF16)
        send(sy.at[part, i], ry.at[part, i], cy_s.at[part, i], cy_r.at[part, i], xdev if part else ydev)

    def half_recv(part, i):
        recv(ry.at[part, i], cy_s.at[part, i], cy_r.at[part, i])

    def r2_first(part):
        half_recv(part, 0)
        for k in range(2):
            ry[part, 0, k] = (ry[part, 0, k].astype(F32) + block(part, k, zat(4), True)).astype(BF16)
        for d in range(2):
            send(ry.at[part, 0, d], r2.at[part, d, 0, d], dz_s.at[part, d, 0], dz_r.at[part, d, 0], zdev[d])

    def r2_hop(part, d, s):
        off = (4 - s if d == 0 else s - 4) % Z
        i = ORDER.index(off)
        half_recv(part, i)
        if s == 1:
            recv(r2.at[part, d, 0, d], dz_s.at[part, d, 0], dz_r.at[part, d, 0])
        else:
            recv(r2.at[part, d, s - 1], dz_s.at[part, d, s - 1], dz_r.at[part, d, s - 1])
        for k in range(2):
            total = ry[part, i, k].astype(F32) + block(part, k, zat(off), True)
            if s > 1 or k == d:
                total = total + r2[part, d, s - 1, k].astype(F32)
            r2[part, d, s - 1, k] = total.astype(BF16)
        send(r2.at[part, d, s - 1], r2.at[part, d, s], dz_s.at[part, d, s], dz_r.at[part, d, s], zdev[d])

    def r2_last(part, k):
        return ((block(part, k, z, True) + ry[part, 7, k].astype(F32))
                + (r2[part, 0, 3, k].astype(F32) + r2[part, 1, 3, k].astype(F32)))

    def r2_end(part):
        half_recv(part, 7)
        for d in range(2):
            recv(r2.at[part, d, 3], dz_s.at[part, d, 3], dz_r.at[part, d, 3])

    cols = (pl.ds(A0, B0 - A0), pl.ds(B0, C0 - B0), pl.ds(C0, DW - C0))

    def owner_copies(part):
        out = []
        if part == 2:
            for yy in range(2):
                out.append((fc.at[yy], xs.at[y, :, :, cols[2]], yy, y, yy, 2 * c + xh))
        else:
            for xl in range(2):
                out.append((fx.at[xl, :, :, cols[part]], xs.at[xh, :, :, cols[part]], xl, xh, y, 2 * c + xl))
        return [o + (jnp.logical_and(jnp.logical_and(o[5] == x, o[4] == y), kx == c),) for o in out]

    def owner_send(part):
        for src, dst, i, j, yt, xo, same in owner_copies(part):
            @pl.when(jnp.logical_not(same))
            def _(src=src, dst=dst, i=i, j=j, yt=yt, xo=xo):
                pltpu.make_async_remote_copy(src_ref=src, dst_ref=dst, send_sem=ex_s.at[part, i],
                                             recv_sem=ex_r.at[part, j], device_id=(2 * hi + kx, fid(z, yt, xo)),
                                             device_id_type=MESH).start()

            @pl.when(same)
            def _(src=src, dst=dst, i=i):
                pltpu.make_async_copy(src, dst, ex_s.at[part, i]).start()

    def owner_wait(part):
        for d in range(2):
            region = xs.at[d, :, :, cols[part]]
            same = jnp.logical_and(jnp.logical_and(is_nat, xh == c), (xh if part < 2 else y) == d)

            @pl.when(jnp.logical_not(same))
            def _(region=region, d=d):
                recv(region, ex_s.at[part, 0], ex_r.at[part, d])
        for src, dst, i, j, yt, xo, same in owner_copies(part):
            @pl.when(jnp.logical_not(same))
            def _(src=src, i=i):
                pltpu.make_async_remote_copy(src_ref=src, dst_ref=src, send_sem=ex_s.at[part, i],
                                             recv_sem=ex_r.at[part, 0], device_id=ydev,
                                             device_id_type=MESH).wait_send()

            @pl.when(same)
            def _(src=src, dst=dst, i=i):
                pltpu.make_async_copy(src, dst, ex_s.at[part, i]).wait()

    grad_a((4, 3, 5))
    rz_first(0, 0, 0, 1, 4)
    rz_first(1, 1, 1, 1, 4)
    rz_first(2, 0, 1, 2, 3)
    rz_first(3, 1, 0, 2, 5)
    grad_c(1 - xh)
    for i in range(8):
        half_send(1, i)
    grad_b(yo)
    for i in range(8):
        half_send(0, i)
    rz_hop(0, 0, 1)
    rz_hop(1, 1, 1)
    grad_a((2, 6, 1, 7, 0))
    rz_hop(0, 1, 2)
    rz_hop(1, 0, 2)
    grad_c(xh)
    r2_first(1)
    rz_hop(0, 0, 2)
    rz_hop(1, 1, 2)
    grad_b(y)
    r2_first(0)
    for part in (1, 0):
        r2_hop(part, 0, 1)
        r2_hop(part, 1, 1)
    rz_hop(0, 1, 3)
    rz_hop(1, 0, 3)
    rz_hop(0, 0, 3)
    rz_hop(1, 1, 3)
    for part in (1, 0):
        r2_hop(part, 0, 2)
        r2_hop(part, 1, 2)
    for d in range(2):
        for k in range(2):
            recv(rz.at[d, k, 3], cz_s.at[d, k, 3], cz_r.at[d, k, 3])
    for k in range(2):
        fs[k] = (grad[k, z, yo, :, :, A0:B0] + rz[0, k, 3, yo].astype(F32)) + rz[1, k, 3, yo].astype(F32)
    send(fs, fr, dy_s.at[0], dy_r.at[0], ydev)
    for k in range(2):
        mine = (grad[k, z, y, :, :, A0:B0] + rz[0, k, 3, y].astype(F32)) + rz[1, k, 3, y].astype(F32)
        for xl in range(2):
            fx[xl, k, :, A0:B0] = mine[xl]
    for part in (1, 0):
        r2_hop(part, 0, 3)
        r2_hop(part, 1, 3)
    recv(fr, dy_s.at[0], dy_r.at[0])
    for k in range(2):
        for xl in range(2):
            fx[xl, k, :, A0:B0] = fx[xl, k, :, A0:B0] + fr[k, xl]
    owner_send(0)
    r2_end(1)
    for k in range(2):
        mine = r2_last(1, k)
        for yy in range(2):
            fc[yy, k] = mine[yy]
    owner_send(2)
    r2_end(0)
    for k in range(2):
        mine = r2_last(0, k)
        for xl in range(2):
            fx[xl, k, :, B0:C0] = mine[xl]
    owner_send(1)
    for part in range(3):
        owner_wait(part)

    scale = inner_rate / math.sqrt(TOKENS)
    for k in range(2):
        inner_o[k] = params[0, :, k, :] - scale * (xs[0, k] + xs[1, k])

    def fragment_of(array):
        pick = [array[:, FRAGW * i:FRAGW * (i + 1)] for i in range(NFRAG)]
        return jnp.where(index == 0, pick[0], jnp.where(index == 1, pick[1], pick[2]))

    for k in range(2):
        osend[k] = fragment_of(inner_o[k])
    for t, dev in enumerate(peers):
        send(osend, orecv.at[t], of_s.at[t], of_r.at[t], dev)
    for t in range(3):
        recv(moms.at[peers[t][0]], om_s.at[t], om_r.at[t])
    moms_o[...] = moms[...]
    for t in range(3):
        recv(orecv.at[t], of_s.at[t], of_r.at[t])
    small[2].wait()
    for k in range(2):
        base = fragment_of(anchor[:, k, :])
        frag_o[k] = (((base - osend[k]) + (base - orecv[0, k])) + ((base - orecv[1, k]) + (base - orecv[2, k]))) * 0.25

    for cp in pending:
        cp.wait_send()


def window(inp, cot, params, anchor, moment, frag):
    dma = pltpu.SemaphoreType.DMA
    vmem = pltpu.VMEM
    both = lambda *shape: [dma(shape), dma(shape)]
    scratch = [
        vmem((2, PAIR, DW), BF16),
        vmem((TOK, DW), BF16),
        vmem((2, Z, Y, 2, ROWS, DW), BF16),
        vmem((2, ROWS, DW), BF16),
        vmem((2, Z, Y, 2, ROWS, PAIR), BF16),
        vmem((2, Z, Y, 2, ROWS, DW), F32),
        vmem((2, 2, 4, Y, 2, ROWS, B0 - A0), BF16),
        vmem((4, Y, 2, ROWS, B0 - A0), BF16),
        vmem((2, 8, 2, 2, ROWS, C0 - B0), BF16),
        vmem((2, 8, 2, 2, ROWS, C0 - B0), BF16),
        vmem((2, 2, 4, 2, 2, ROWS, C0 - B0), BF16),
        vmem((2, 2, ROWS, B0 - A0), F32),
        vmem((2, 2, ROWS, B0 - A0), F32),
        vmem((2, 2, ROWS, DW - C0), F32),
        vmem((2, 2, ROWS, DW), F32),
        vmem((2, 2, ROWS, DW), F32),
        vmem((2, ROWS, FRAGW), F32),
        vmem((3, 2, ROWS, FRAGW), F32),
        vmem((4, 2, ROWS, QUARTER), F32),
        vmem((1, ROWS, 2, DW), F32),
        vmem((ROWS, 2, DW), F32),
        vmem((NFRAG, ROWS, 2, QUARTER), F32),
        dma((3,)),
        dma((2, 6)),
        dma((2, 6)), dma((2, 9)),
        *both(2, 3),
        *both(2, 2),
        *both(1),
        *both(2, 2, 4),
        *both(2, 4),
        *both(9),
        *both(2, 2, 4),
        *both(2, 8),
        *both(2, 2, 4),
        *both(1),
        *both(3, 2),
        *both(3),
        *both(3),
    ]
    whole = pl.BlockSpec(memory_space=pltpu.VMEM)
    return pl.pallas_call(
        kernel,
        out_shape=(
            jax.ShapeDtypeStruct((2, ROWS, DW), F32),
            jax.ShapeDtypeStruct((2, ROWS, FRAGW), F32),
            jax.ShapeDtypeStruct((4, 2, ROWS, QUARTER), F32),
        ),
        in_specs=[pl.BlockSpec(memory_space=pl.ANY)] * 5 + [pl.BlockSpec(memory_space=pltpu.SMEM)],
        out_specs=(whole, whole, whole),
        scratch_shapes=scratch,
        cost_estimate=pl.CostEstimate(flops=4 * 2 * TOK * DW * HV, bytes_accessed=10**7, transcendentals=TOK),
        compiler_params=pltpu.CompilerParams(
            collective_id=1, has_side_effects=True, vmem_limit_bytes=58 * 2**20
        ),
    )(inp, cot, params, anchor, moment, frag)


def finish(frag, inner, delta, moms, anchor, moment, replica_o, anchor_o, moment_o):
    index = frag[0]
    rep = lax.axis_index("rep")
    anchor_o[...] = anchor[...]
    moment_o[...] = moment[...]
    for k in range(2):
        change = delta[k]
        base = anchor[:, k, :]
        pick = [base[:, FRAGW * i:FRAGW * (i + 1)] for i in range(NFRAG)]
        base = jnp.where(index == 0, pick[0], jnp.where(index == 1, pick[1], pick[2]))
        old = jnp.concatenate([moms[r, k] for r in range(4)], axis=-1)
        new_moment = outer_momentum * old + change
        new_frag = base - outer_rate * (change + outer_momentum * new_moment)
        replica_o[0, :, k, :] = inner[k]
        for i in range(NFRAG):
            @pl.when(index == i)
            def _(i=i):
                replica_o[0, :, k, FRAGW * i:FRAGW * (i + 1)] = new_frag
                anchor_o[:, k, FRAGW * i:FRAGW * (i + 1)] = new_frag
        part = [new_moment[:, QUARTER * i:QUARTER * (i + 1)] for i in range(4)]
        low = jnp.where(rep == 0, part[0], part[1])
        high = jnp.where(rep == 2, part[2], part[3])
        moment_o[index, :, k, :] = jnp.where(rep < 2, low, high)


def per_device(inputs, cotangent, replica_params, anchor, momentum, fragment):
    inner, delta, moms = window(inputs, cotangent, replica_params, anchor, momentum, fragment)
    whole = pl.BlockSpec(memory_space=pltpu.VMEM)
    return pl.pallas_call(
        finish,
        out_shape=(
            jax.ShapeDtypeStruct((1, ROWS, 2, DW), F32),
            jax.ShapeDtypeStruct((ROWS, 2, DW), F32),
            jax.ShapeDtypeStruct((NFRAG, ROWS, 2, QUARTER), F32),
        ),
        in_specs=[pl.BlockSpec(memory_space=pltpu.SMEM)] + [whole] * 5,
        out_specs=(whole, whole, whole),
    )(fragment, inner, delta, moms, anchor, momentum)


def solution(mesh):
    return jax.shard_map(
        per_device,
        mesh=mesh,
        in_specs=(
            P("rep", "fsdp", None),
            P("rep", "fsdp", None),
            P("rep", "fsdp", None, None),
            P("fsdp", None, None),
            P(None, "fsdp", None, "rep"),
            P(),
        ),
        out_specs=(
            P("rep", "fsdp", None, None),
            P("fsdp", None, None),
            P(None, "fsdp", None, "rep"),
        ),
        check_vma=False,
    )
```
